32 devices in a mesh: groups: 2 (over x), tokens: 16 (over z, y, core).
Axes of the slice: x: 2, y: 2, z: 4, core: 2. Of those that a mesh axis runs over, the one named last changes fastest.
Arguments:
- update_keys: bfloat16 [16384, 2048], P(('groups', 'tokens')), parts along dimension 0, may hold values from -6 to 6
- update_values: bfloat16 [16384, 2048], P(('groups', 'tokens')), parts along dimension 0, may hold values from -6 to 6
- update_rates: float32 [16384, 4], P(('groups', 'tokens')), parts along dimension 0, may hold values from 0.05 to 1
- update_mask: int32 [16384], P(('groups', 'tokens')), parts along dimension 0, may hold values 0 or 1
- fast_weights: bfloat16 [4, 3, 512, 512], replicated, may hold values from -0.25 to 0.25
- step_sizes: float32 [4], replicated, may hold values from 0.02 to 0.08
- target_queries: bfloat16 [4096, 2048], P(('groups', 'tokens')), parts along dimension 0, may hold values from -8 to 8
- target_keys: bfloat16 [4096, 2048], P(('groups', 'tokens')), parts along dimension 0, may hold values from -8 to 8
- target_values: bfloat16 [4096, 2048], P(('groups', 'tokens')), parts along dimension 0, may hold values from -6 to 6
- target_views: int32 [4096], P(('groups', 'tokens')), parts along dimension 0, may hold values from 0 to 15, as said below
Outputs:
- mixed: bfloat16 [4096, 2048], P(('groups', 'tokens')), parts along dimension 0
The draws below stay inside these ranges and needn't reach their ends.
There are 2 independent parts, one for each index of `groups`. The reference program is written for one: setup_inputs(seed, part) draws one part's arguments, and reference() takes and returns one part's arrays. A program takes and returns all parts, laid end to end along the dimension named above; an argument that names none is the same for every part. Nothing has to cross between parts.
Inputs may be any that keep to these rules, and one draw needn't show every extreme that they name: `target_views`: every view id names exactly 128 rows. Owner o holds view o; of the 128 rows of one device, either none or exactly 16 belong to the view of one owner.
All inputs are finite; a program needn't handle non-finite values. No bound on the sum of `update_mask` on one device may be relied on, other than what follows from the above.
Results may differ from the reference program's by a relative error of at most 0.0083.
Values may be sent and summed in bfloat16 or wider, within the bound.
No kernel may reach another device: no remote copies, remote signals or barrier semaphores. Data moves between devices by JAX's collectives and lax.ppermute only.
A program may use at most 128 MiB of HBM per device.

```python
import math
import jax
import jax.numpy as jnp
from jax import lax

HEADS = 4
DH = 512
VIEW_ROWS = 128
UPD_DEV = 512
VIEWS_DEV = 1
WIDTH = 2048
TGT_DEV = 128
CAP = 16
UPD_ROWS = 8192
TGT_ROWS = 2048
VIEWS = 16
N_TOKENS = 16


def view_layout(key):
    dev_count = TGT_ROWS // TGT_DEV
    half_count = dev_count // 2
    offsets = jax.random.permutation(jax.random.fold_in(key, 11), dev_count)[:half_count]
    source_dev = jnp.arange(dev_count, dtype=jnp.int32)[:, None]
    dest_pairs = (source_dev + offsets[None, :].astype(jnp.int32)) % dev_count
    dest_dev = jnp.repeat(dest_pairs, CAP, axis=1)
    incoming = jnp.broadcast_to(jnp.arange(TGT_DEV, dtype=jnp.int32)[None, :], (dev_count, TGT_DEV))
    arrival = jax.vmap(lambda sub_key: jax.random.permutation(sub_key, TGT_DEV))(jax.random.split(jax.random.fold_in(key, 12), dev_count))
    local_view = arrival[dest_dev, incoming].astype(jnp.int32) // VIEW_ROWS
    view_ids = dest_dev * VIEWS_DEV + local_view
    shuffle = jax.vmap(lambda sub_key: jax.random.permutation(sub_key, TGT_DEV))(jax.random.split(jax.random.fold_in(key, 13), dev_count))
    view_ids = jnp.take_along_axis(view_ids, shuffle.astype(jnp.int32), axis=1)
    return view_ids.reshape(-1).astype(jnp.int32)


def draw_target_views(key, part):
    return view_layout(key)


def drawn_pair(key):
    shape = (TGT_ROWS, WIDTH)
    queries = jnp.clip(jax.random.normal(jax.random.fold_in(key, 27), shape, jnp.float32), -4.0, 4.0)
    keys_out = jnp.clip(jax.random.normal(jax.random.fold_in(key, 28), shape, jnp.float32), -4.0, 4.0)
    return (queries, keys_out)


def draw_target_queries(key, part):
    return drawn_pair(key)[0].astype(jnp.bfloat16)


def draw_target_keys(key, part):
    return drawn_pair(key)[1].astype(jnp.bfloat16)


def touch_ends(result, stream_key, smallest, high):
    index_at = [jax.random.randint(jax.random.fold_in(stream_key, axis), (), 0, length) for axis, length in enumerate(result.shape)]
    main_axis = result.shape.index(max(result.shape))
    neighbour = index_at[:main_axis] + [(index_at[main_axis] + 1) % result.shape[main_axis]] + index_at[main_axis + 1:]
    return result.at[tuple(index_at)].set(smallest).at[tuple(neighbour)].set(high)


def raised(entries, key, source, target, shards_of, factor):
    def block_of(axis_at):
        return (jnp.arange(entries.shape[axis_at]) // (entries.shape[axis_at] // shards_of)).reshape((-1,) + (1,) * (entries.ndim - 1 - axis_at))

    near = jax.random.permutation(key, shards_of)[block_of(target)]
    far = (block_of(target) + shards_of // 2) % shards_of
    return jnp.where((block_of(source) == near) | (block_of(source) == far), factor * entries, entries)


def block_scale(key, shape, cuts, smallest, largest):
    def one(axis_at, shards_of):
        draws = jax.random.uniform(jax.random.fold_in(jax.random.fold_in(key, 6), axis_at), (shards_of,), jnp.float32, smallest / len(cuts), largest / len(cuts))
        return jnp.repeat(jnp.exp(draws), shape[axis_at] // shards_of).reshape((-1,) + (1,) * (len(shape) - axis_at - 1))

    level = one(*cuts[0])
    for cut in cuts[1:]:
        level = level * one(*cut)
    return level


def bell_draw(stream_key, dims, width, reach, pieces=(), held_as=jnp.bfloat16):
    entries = jax.random.normal(stream_key, dims, jnp.float32) * width
    if len(pieces) > 0:
        entries = block_scale(stream_key, dims, pieces, -0.22, 0.18) * entries
    return jnp.clip(entries, min=-reach, max=reach).astype(held_as)


def heavy_noise(stream_key, dims, deviation, limit, pieces, heavy, held_as=jnp.bfloat16):
    values = deviation * jax.random.normal(stream_key, dims, jnp.float32)
    if pieces:
        values = values * block_scale(stream_key, dims, pieces, -0.22, 0.18)
    return jnp.clip(raised(values, jax.random.fold_in(stream_key, 3), *heavy), -limit, limit).astype(held_as)


def setup_inputs(seed: int = 0, part: int = 0) -> dict:
    key_list = jax.random.split(jax.random.key(seed), 11)
    own_keys = jax.random.split(jax.random.fold_in(key_list[10], part), 11)
    update_keys = heavy_noise(own_keys[0], (UPD_ROWS, WIDTH), 1.0, 6.0, ((0, 16),), (0, 1, 16, 2.0))
    update_values = bell_draw(own_keys[1], (UPD_ROWS, WIDTH), 1.0, 6.0, ((0, 16),))
    update_rates = jnp.clip(jnp.exp(math.log(1.0) - 2.9957323 * jax.random.uniform(own_keys[2], (UPD_ROWS, HEADS), jnp.float32) ** block_scale(own_keys[2], (UPD_ROWS, HEADS), ((0, 16),), -0.2, 0.2)), 0.05, 1.0)
    update_mask = touch_ends((jax.random.randint(own_keys[3], (UPD_ROWS,), 0, 4) < 3).astype(jnp.int32), jax.random.fold_in(own_keys[3], 1), 0, 1)
    fast_weights = bell_draw(key_list[4], (HEADS, 3, DH, DH), DH ** -0.5, 0.25)
    step_sizes = jnp.clip(jnp.exp(jax.random.uniform(key_list[5], (HEADS,), jnp.float32, math.log(0.02), math.log(0.08))), 0.02, 0.08)
    target_queries = draw_target_queries(jax.random.fold_in(jax.random.fold_in(key_list[10], part), 71), part)
    target_keys = draw_target_keys(jax.random.fold_in(jax.random.fold_in(key_list[10], part), 71), part)
    target_values = bell_draw(own_keys[8], (TGT_ROWS, WIDTH), 1.0, 6.0, ((0, 16),))
    target_views = draw_target_views(jax.random.fold_in(jax.random.fold_in(key_list[10], part), 71), part)
    return dict(update_keys=update_keys, update_values=update_values, update_rates=update_rates, update_mask=update_mask, fast_weights=fast_weights, step_sizes=step_sizes, target_queries=target_queries, target_keys=target_keys, target_values=target_values, target_views=target_views)


epsilon = 1e-05
highest = lax.Precision.HIGHEST

def rounded(values):
    return lax.optimization_barrier(values.astype(jnp.bfloat16)).astype(jnp.float32)

def swish_parts(pre_gate):
    sigma = jax.nn.sigmoid(pre_gate)
    return (pre_gate * sigma, sigma * (1.0 + pre_gate * (1.0 - sigma)))

def row_normalize(matrix):
    return matrix * lax.rsqrt(lax.optimization_barrier(jnp.mean(matrix * matrix, axis=-1, keepdims=True)) + epsilon)

def reference(update_keys, update_values, update_rates, update_mask, fast_weights, step_sizes, target_queries, target_keys, target_values, target_views):
    weights = fast_weights.astype(jnp.float32)
    keep_rates = update_mask.astype(jnp.float32)[:, None] * update_rates

    def accumulate(block_index, grad_sum):
        first_row = (block_index * UPD_DEV).astype(jnp.int32)
        key_rows = lax.dynamic_slice_in_dim(update_keys, first_row, UPD_DEV, 0).astype(jnp.float32).reshape(UPD_DEV, HEADS, DH)
        value_rows = lax.dynamic_slice_in_dim(update_values, first_row, UPD_DEV, 0).astype(jnp.float32).reshape(UPD_DEV, HEADS, DH)
        rate_rows = lax.dynamic_slice_in_dim(keep_rates, first_row, UPD_DEV, 0)
        target_grad = rounded(-rate_rows[:, :, None] * value_rows)
        pre_gate = jnp.einsum('rhi,hij->rhj', key_rows, weights[:, 0], precision=highest)
        pre_up = jnp.einsum('rhi,hij->rhj', key_rows, weights[:, 1], precision=highest)
        activated, slope = swish_parts(pre_gate)
        hidden = rounded(activated * pre_up)
        back = jnp.einsum('rho,hjo->rhj', target_grad, weights[:, 2], precision=highest)
        grad_gate = rounded(back * pre_up * slope)
        grad_up = rounded(back * activated)
        gate_term = jnp.einsum('rhi,rhj->hij', key_rows, grad_gate, precision=highest)
        up_term = jnp.einsum('rhi,rhj->hij', key_rows, grad_up, precision=highest)
        down_term = jnp.einsum('rhj,rho->hjo', hidden, target_grad, precision=highest)
        return grad_sum + jnp.stack([gate_term, up_term, down_term], axis=1)
    gradient = lax.fori_loop(0, N_TOKENS, accumulate, jnp.zeros((HEADS, 3, DH, DH), jnp.float32))
    fresh = rounded(weights - step_sizes[:, None, None, None] * row_normalize(gradient))
    view_hit = (target_views[:, None] == jnp.arange(VIEWS, dtype=jnp.int32)[None, :]).astype(jnp.int32)
    within_view = lax.optimization_barrier(jnp.sum(view_hit * (jnp.cumsum(view_hit, axis=0) - 1), axis=1))
    position = (target_views * VIEW_ROWS + within_view).astype(jnp.int32)
    arranged = [jnp.zeros_like(source_rows).at[position].set(source_rows) for source_rows in (target_queries, target_keys, target_values)]
    query_rows = arranged[0].astype(jnp.float32).reshape(TGT_ROWS, HEADS, DH)
    pre_gate = jnp.einsum('rhi,hij->rhj', query_rows, fresh[:, 0], precision=highest)
    pre_up = jnp.einsum('rhi,hij->rhj', query_rows, fresh[:, 1], precision=highest)
    activated, slope = swish_parts(pre_gate)
    target_hidden = rounded(activated * pre_up)
    fast_out = jnp.einsum('rhj,hjo->rho', target_hidden, fresh[:, 2], precision=highest)
    normed = row_normalize(fast_out)
    view_shape = (VIEWS, VIEW_ROWS, HEADS, DH)
    view_queries = arranged[0].astype(jnp.float32).reshape(view_shape)
    view_keys = arranged[1].astype(jnp.float32).reshape(view_shape)
    view_values = arranged[2].astype(jnp.float32).reshape(view_shape)
    scores = jnp.einsum('vqhd,vkhd->vhqk', view_queries, view_keys, precision=highest) * DH ** (-0.5)
    probs = rounded(jax.nn.softmax(scores, axis=-1))
    attended = jnp.einsum('vhqk,vkhd->vqhd', probs, view_values, precision=highest).reshape(TGT_ROWS, HEADS, DH)
    return (normed + attended).reshape(TGT_ROWS, WIDTH).astype(jnp.bfloat16)
```

```python
import jax
import jax.numpy as jnp
from jax import lax
from jax.sharding import PartitionSpec as P

VIEW_ROWS = 128
AXIS = "tokens"
epsilon = 1e-05
f32 = jnp.float32
bf16 = jnp.bfloat16


def row_normalize(matrix):
    return matrix * lax.rsqrt(jnp.mean(matrix * matrix, axis=-1, keepdims=True) + epsilon)


def swap(value, mask, senders=None):
    count = lax.axis_size(AXIS)
    pairs = [(t, t ^ mask) for t in range(count) if senders is None or senders(t)]
    return lax.ppermute(value, AXIS, pairs)


def head_of(plane, head_count):
    half = head_count // 2
    return (plane % 2) * half + plane // 2


def head_partials(keys, grads, weights, bit):
    pre_gate = jnp.dot(keys, weights[0], preferred_element_type=f32)
    pre_up = jnp.dot(keys, weights[1], preferred_element_type=f32)
    back = lax.dot_general(grads, weights[2], (((1,), (1,)), ((), ())), preferred_element_type=f32)
    sigma = jax.nn.sigmoid(pre_gate)
    activated = pre_gate * sigma
    hidden = (activated * pre_up).astype(bf16)
    grad_gate = (back * pre_up * (sigma * (1.0 + pre_gate * (1.0 - sigma)))).astype(bf16)
    grad_up = (back * activated).astype(bf16)
    out = []
    for left, right in ((keys, grad_gate), (keys, grad_up), (hidden, grads)):
        full = lax.dot_general(
            left, right, (((0,), (0,)), ((), ())), preferred_element_type=f32
        ).astype(bf16)
        rows = full.shape[0] // 2
        keep = lax.dynamic_slice_in_dim(full, bit * rows, rows, 0)
        send = lax.dynamic_slice_in_dim(full, (1 - bit) * rows, rows, 0)
        out.append((send, keep))
    return out


def on_device(
    update_keys,
    update_values,
    update_rates,
    update_mask,
    fast_weights,
    step_sizes,
    target_queries,
    target_keys,
    target_values,
    target_views,
):
    heads, _, width, _ = fast_weights.shape
    count = lax.axis_size(AXIS)
    me = lax.axis_index(AXIS)
    span = count // heads
    plane, inner = me // span, me % span
    core = inner % 2
    half = heads // 2
    inner_bits = [b for b in range(1, span.bit_length() - 1)]
    my_head = head_of(plane, heads)
    bit_of = lambda b: (me >> b) & 1
    first_bit = bit_of(1)

    rates = -(update_mask.astype(f32)[:, None] * update_rates)

    def grads_of(which):
        cols = lax.dynamic_slice_in_dim(update_values, which * half * width, half * width, 1)
        rate = lax.dynamic_slice_in_dim(rates, which * half, half, 1)
        rows = cols.shape[0]
        scaled = rate[:, :, None] * cols.reshape(rows, half, width).astype(f32)
        return scaled.reshape(rows, half * width).astype(bf16)

    def keys_of(which):
        return lax.dynamic_slice_in_dim(update_keys, which * half * width, half * width, 1)

    keys_in = swap(keys_of(1 - core), 1)
    grads_in = swap(grads_of(1 - core), 1)
    keys_all = jnp.concatenate([keys_of(core), keys_in], axis=0)
    grads_all = jnp.concatenate([grads_of(core), grads_in], axis=0)

    def rows_for(dest):
        head = head_of(dest, heads)
        return jnp.stack(
            [
                lax.dynamic_slice_in_dim(x, head * width, width, 1)
                for x in (target_queries, target_keys, target_values)
            ]
        )

    pieces = []
    for step in range(heads):
        piece = rows_for(plane ^ step)
        if step:
            piece = swap(piece, step * span)
        group = [(0, piece)]
        for b in reversed([0] + inner_bits):
            group = group + [(e | (1 << b), swap(x, 1 << b)) for e, x in group]
        pieces.append([x for _, x in sorted(group, key=lambda item: item[0])])

    views = lax.all_gather(target_views, AXIS, axis=0, tiled=True)
    mine = (views % span) == inner
    view_hit = (
        mine[:, None] & ((views // span)[:, None] == jnp.arange(heads, dtype=jnp.int32)[None, :])
    ).astype(jnp.int32)
    rank = jnp.sum(view_hit * (jnp.cumsum(view_hit, axis=0) - 1), axis=1)
    place = jnp.where(mine, (views // span) * VIEW_ROWS + rank, -1)
    bits = count.bit_length() - 1
    place = place.reshape((2,) * bits + (-1,))
    for b in range(bits):
        place = jnp.where(bit_of(b) == 1, jnp.flip(place, axis=bits - 1 - b), place)
    place = place.reshape(-1)
    pick = (
        jnp.arange(heads * VIEW_ROWS, dtype=jnp.int32)[:, None] == place[None, :]
    ).astype(bf16)
    gathered = jnp.concatenate([x for group in pieces for x in group], axis=1)
    arranged = [
        jnp.dot(pick, gathered[i], preferred_element_type=f32).astype(bf16) for i in range(3)
    ]

    fresh_parts = []
    reduced = {}
    for j in range(half):
        head = core * half + j
        weights = lax.dynamic_index_in_dim(fast_weights, head, 0, keepdims=False)
        cols = slice(j * width, (j + 1) * width)
        parts = head_partials(keys_all[:, cols], grads_all[:, cols], weights, first_bit)
        for i in (2, 0, 1):
            send, keep = parts[i]
            total = keep.astype(f32) + swap(send, 2).astype(f32)
            for b in inner_bits[1:]:
                rows = total.shape[0] // 2
                send = lax.dynamic_slice_in_dim(total, (1 - bit_of(b)) * rows, rows, 0)
                keep = lax.dynamic_slice_in_dim(total, bit_of(b) * rows, rows, 0)
                total = keep + swap(send.astype(bf16), 1 << b).astype(f32)
            total = total + swap(
                total.astype(bf16), span, lambda t: (t // span) % 2 != t % 2
            ).astype(f32)
            for b in range(1, heads.bit_length() - 1):
                mask = 1 << (b - 1)
                total = total + swap(
                    total.astype(bf16),
                    span << b,
                    lambda t: (t // span) % 2 == t % 2
                    and ((t // span) // 2 % (2 * mask)) == ((j % (2 * mask)) ^ mask),
                ).astype(f32)
            reduced[j, i] = total

    share_rows = reduced[0, 0].shape[0]
    first_row = jnp.int32(0)
    for b in inner_bits:
        first_row = first_row * 2 + bit_of(b)
    first_row = first_row * share_rows
    owner = lambda t: (t // span) % 2 == t % 2
    is_owner = (plane % 2) == core
    step_size = lax.dynamic_index_in_dim(step_sizes, my_head, 0, keepdims=False)
    fresh = []
    for i in range(3):
        total = reduced[0, i]
        for j in range(1, half):
            total = jnp.where(plane // 2 == j, reduced[j, i], total)
        old = lax.dynamic_slice(
            fast_weights, (my_head, i, first_row, 0), (1, 1, share_rows, width)
        ).reshape(share_rows, width)
        new = (old.astype(f32) - step_size * row_normalize(total)).astype(bf16)
        for b in reversed(inner_bits):
            other = swap(new, 1 << b, owner)
            new = jnp.where(
                bit_of(b) == 1,
                jnp.concatenate([other, new], axis=0),
                jnp.concatenate([new, other], axis=0),
            )
        other = swap(new, 1, owner)
        fresh.append(jnp.where(is_owner, new, other))

    view_shape = (heads, VIEW_ROWS, width)
    scores = jnp.einsum(
        "vqd,vkd->vqk",
        arranged[0].reshape(view_shape),
        arranged[1].reshape(view_shape),
        preferred_element_type=f32,
    ) * width ** (-0.5)
    probs = jax.nn.softmax(scores, axis=-1).astype(bf16)
    attended = jnp.einsum(
        "vqk,vkd->vqd", probs, arranged[2].reshape(view_shape), preferred_element_type=f32
    ).reshape(heads * VIEW_ROWS, width)
    pre_gate = jnp.dot(arranged[0], fresh[0], preferred_element_type=f32)
    pre_up = jnp.dot(arranged[0], fresh[1], preferred_element_type=f32)
    hidden = (jax.nn.sigmoid(pre_gate) * pre_gate * pre_up).astype(bf16)
    fast_out = jnp.dot(hidden, fresh[2], preferred_element_type=f32)
    mixed = (row_normalize(fast_out) + attended).astype(bf16).reshape(view_shape)

    got = []
    for step in range(heads):
        block = lax.dynamic_index_in_dim(mixed, plane ^ step, 0, keepdims=False)
        got.append(swap(block, step * span) if step else block)
    columns = []
    for head in range(heads):
        source = (head % half) * 2 + head // half
        column = got[0]
        for step in range(1, heads):
            column = jnp.where((plane ^ step) == source, got[step], column)
        columns.append(column)
    return jnp.concatenate(columns, axis=1)


def solution(mesh):
    rows = P(("groups", "tokens"), None)
    return jax.shard_map(
        on_device,
        mesh=mesh,
        in_specs=(
            rows,
            rows,
            rows,
            P(("groups", "tokens")),
            P(),
            P(),
            rows,
            rows,
            rows,
            P(("groups", "tokens")),
        ),
        out_specs=rows,
        check_vma=False,
    )
```

```python
import functools

import jax
import jax.numpy as jnp
from jax import lax
from jax.experimental import pallas as pl
from jax.experimental.pallas import tpu as pltpu
from jax.sharding import PartitionSpec as P

VIEW_ROWS = 128
AXIS = "tokens"
epsilon = 1e-05
f32 = jnp.float32
bf16 = jnp.bfloat16
i32 = jnp.int32
TAG_ROWS = 16
VMEM_LIMIT = 48 * 1024 * 1024


def swap(value, mask, senders=None):
    count = lax.axis_size(AXIS)
    pairs = [(t, t ^ mask) for t in range(count) if senders is None or senders(t)]
    return lax.ppermute(value, AXIS, pairs)


def head_of(plane, head_count):
    half = head_count // 2
    return (plane % 2) * half + plane // 2


def whole(shape):
    return pl.BlockSpec(shape, lambda *_: (0,) * len(shape))


def call(body, name, scalars, inputs, specs, outs, grid=(1,), out_specs=None, scratch=(), flops=0):
    moved = sum(x.size * x.dtype.itemsize for x in inputs) + sum(
        x.size * x.dtype.itemsize for x in outs
    )
    return pl.pallas_call(
        body,
        name=name,
        grid_spec=pltpu.PrefetchScalarGridSpec(
            num_scalar_prefetch=1,
            grid=grid,
            in_specs=specs,
            out_specs=out_specs or [whole(o.shape) for o in outs],
            scratch_shapes=list(scratch),
        ),
        out_shape=list(outs),
        cost_estimate=pl.CostEstimate(flops=flops, bytes_accessed=moved, transcendentals=0),
        compiler_params=pltpu.CompilerParams(vmem_limit_bytes=VMEM_LIMIT),
    )(scalars, *inputs)


def lane_pick(table, lane):
    at = lax.broadcasted_iota(i32, table.shape, 1) == lane
    return jnp.sum(jnp.where(at, table, 0.0), axis=1, keepdims=True)


def pack_update_body(half, width, where, keys, values, rates, out):
    other = 1 - where[1]
    out[0] = keys[...]
    for j in range(half):
        cols = pl.ds(j * width, width)
        rate = lane_pick(rates[...], other * half + j)
        out[1, :, cols] = (rate * values[:, cols].astype(f32)).astype(bf16)


def pack_update(where, keys, values, rates, half, width):
    rows, cols = keys.shape[0], half * width
    block = min(128, rows)
    spec = pl.BlockSpec((block, cols), lambda i, w: (i, 1 - w[1]))
    return call(
        functools.partial(pack_update_body, half, width),
        "pack_update",
        where,
        (keys, values, rates),
        [spec, spec, pl.BlockSpec((block, rates.shape[1]), lambda i, w: (i, 0))],
        [jax.ShapeDtypeStruct((2, rows, cols), bf16)],
        grid=(rows // block,),
        out_specs=[pl.BlockSpec((2, block, cols), lambda i, w: (0, i, 0))],
    )[0]


def pack_target_body(heads, width, where, queries, keys, values, tags, *outs):
    rows = queries.shape[0]
    for step in range(heads):
        head = head_of(where[0] ^ step, heads)
        cols = pl.ds(pl.multiple_of(head * width, width), width)
        for i, source in enumerate((queries, keys, values)):
            outs[step][pl.ds(i * rows, rows), :] = source[:, cols]
        outs[step][pl.ds(3 * rows, TAG_ROWS), :] = jnp.zeros((TAG_ROWS, width), bf16)
        outs[step][pl.ds(3 * rows, TAG_ROWS), pl.ds(0, rows)] = tags[...]


def pack_target(where, queries, keys, values, tags, heads, width):
    rows = queries.shape[0]
    out = jax.ShapeDtypeStruct((3 * rows + TAG_ROWS, width), bf16)
    inputs = (queries, keys, values, tags)
    return call(
        functools.partial(pack_target_body, heads, width),
        "pack_target",
        where,
        inputs,
        [whole(x.shape) for x in inputs],
        [out] * heads,
    )


def head_grad_body(lane, half, where, keys, values, rates, other, weights, *refs):
    sends, keeps = refs[:2], refs[2:4]
    hidden_s, gate_s, up_s, grads_s, full = refs[4:]
    rows, width = keys.shape
    head = where[1] * half + lane
    chunk = 256
    for at in range(0, 2 * rows, chunk):
        span = pl.ds(at, chunk)
        if at < rows:
            k = keys[span, :]
            rate = lane_pick(rates[span, :], head)
            tg = (rate * values[span, :].astype(f32)).astype(bf16)
        else:
            k = other[0, pl.ds(at - rows, chunk), :]
            tg = other[1, pl.ds(at - rows, chunk), :]
        grads_s[span, :] = tg
        pre_gate = jnp.dot(k, weights[0, 0], preferred_element_type=f32)
        pre_up = jnp.dot(k, weights[0, 1], preferred_element_type=f32)
        back = lax.dot_general(
            tg, weights[0, 2], (((1,), (1,)), ((), ())), preferred_element_type=f32
        )
        sigma = jax.nn.sigmoid(pre_gate)
        activated = pre_gate * sigma
        hidden_s[span, :] = (activated * pre_up).astype(bf16)
        gate_s[span, :] = (back * pre_up * (sigma * (1.0 + pre_gate * (1.0 - sigma)))).astype(bf16)
        up_s[span, :] = (back * activated).astype(bf16)
    outer = (((0,), (0,)), ((), ()))
    upper = pl.ds(0, rows)
    lower = pl.ds(rows, rows)
    for i, right in enumerate((gate_s, up_s)):
        full[i] = lax.dot_general(
            keys[...], right[upper, :], outer, preferred_element_type=f32
        ) + lax.dot_general(other[0], right[lower, :], outer, preferred_element_type=f32)
    full[2] = lax.dot_general(hidden_s[...], grads_s[...], outer, preferred_element_type=f32)
    quarter = width // 4
    bit = where[2]
    for g in range(2):
        for i in range(3):
            kept = pl.ds(pl.multiple_of(bit * 2 * quarter + g * quarter, quarter), quarter)
            sent = pl.ds(pl.multiple_of((1 - bit) * 2 * quarter + g * quarter, quarter), quarter)
            keeps[g][i] = full[i, kept, :]
            sends[g][i] = full[i, sent, :].astype(bf16)


def head_grad(where, keys, values, rates, other, weights, lane, half, width):
    rows = keys.shape[0]
    own = pl.BlockSpec((rows, width), lambda i, w: (0, w[1] * half + lane))
    shape = (3, width // 4, width)
    both = pltpu.VMEM((2 * rows, width), bf16)
    outs = call(
        functools.partial(head_grad_body, lane, half),
        "head_grad_%d" % lane,
        where,
        (keys, values, rates, other, weights),
        [
            own,
            own,
            whole(rates.shape),
            pl.BlockSpec((2, rows, width), lambda i, w: (0, 0, lane)),
            pl.BlockSpec((1, 3, width, width), lambda i, w: (w[1] * half + lane, 0, 0, 0)),
        ],
        [jax.ShapeDtypeStruct(shape, bf16)] * 2 + [jax.ShapeDtypeStruct(shape, f32)] * 2,
        scratch=[both] * 4 + [pltpu.VMEM((3, width, width), f32)],
        flops=24 * rows * width * width,
    )
    return outs[:2], outs[2:]


def arrange_body(count, span, where, *refs):
    pieces, outs = refs[:-2], refs[-2:]
    me = where[3]
    inner = where[4]
    rows = (pieces[0].shape[0] - TAG_ROWS) // 3
    heads = count // span
    core = inner % 2
    tags = [p[pl.ds(3 * rows, TAG_ROWS), pl.ds(0, rows)].astype(f32) for p in pieces]
    ids = jnp.concatenate(
        [t[0:1, :] * 256.0 + t[1:2, :] for t in tags]
        + [t[2:3, :] * 256.0 + t[3:4, :] for t in tags],
        axis=0,
    ).astype(i32)
    own = len(pieces)

    def source_of(shape, axis):
        index = lax.broadcasted_iota(i32, shape, axis)
        diff = jnp.where(index < own, 2 * index, 2 * (index - own) + 1)
        return me ^ diff

    earlier = (source_of((count, count), 1) < source_of((count, count), 0)).astype(f32)
    before = (
        lax.broadcasted_iota(i32, (rows, rows), 0) < lax.broadcasted_iota(i32, (rows, rows), 1)
    ).astype(f32)
    for which, out in enumerate(outs):
        target = inner - core + (core if which == 0 else 1 - core)
        place = jnp.full((count, rows), -1.0, f32)
        for j in range(heads):
            hit = (ids == j * span + target).astype(f32)
            rank = jnp.dot(hit, before, preferred_element_type=f32) + jnp.sum(
                jnp.dot(earlier, hit, preferred_element_type=f32), axis=1, keepdims=True
            )
            place = jnp.where(hit > 0.0, rank + float(j * VIEW_ROWS), place)
        place = place.astype(i32)
        group = 4
        totals = [None] * 3
        for first in range(0, own, group):
            row_at = lax.broadcasted_iota(i32, (heads * VIEW_ROWS, rows), 0)
            pick = jnp.concatenate(
                [
                    (row_at == place[n : n + 1, :]).astype(f32).astype(bf16)
                    for n in range(first, first + group)
                ],
                axis=1,
            )
            for i in range(3):
                source = jnp.concatenate(
                    [pieces[n][pl.ds(i * rows, rows), :] for n in range(first, first + group)],
                    axis=0,
                )
                part = jnp.dot(pick, source, preferred_element_type=f32)
                totals[i] = part if totals[i] is None else totals[i] + part
        for i in range(3):
            out[i] = totals[i].astype(bf16)


def arrange(where, pieces, count, span, heads, width):
    shape = jax.ShapeDtypeStruct((3, heads * VIEW_ROWS, width), bf16)
    return call(
        functools.partial(arrange_body, count, span),
        "arrange",
        where,
        tuple(pieces),
        [whole(x.shape) for x in pieces],
        [shape] * 2,
        flops=12 * VIEW_ROWS * heads * width * VIEW_ROWS * len(pieces),
    )


def attend_body(where, own, other, queries, attended):
    width = queries.shape[1]
    q = own[0] + other[0]
    queries[...] = q
    for v in range(q.shape[0] // VIEW_ROWS):
        at = pl.ds(v * VIEW_ROWS, VIEW_ROWS)
        k = own[1, at, :] + other[1, at, :]
        scores = lax.dot_general(
            own[0, at, :] + other[0, at, :],
            k,
            (((1,), (1,)), ((), ())),
            preferred_element_type=f32,
        ) * width ** (-0.5)
        top = jnp.max(scores, axis=1, keepdims=True)
        raised = jnp.exp(scores - top)
        probs = (raised / jnp.sum(raised, axis=1, keepdims=True)).astype(bf16)
        attended[at, :] = jnp.dot(
            probs, own[2, at, :] + other[2, at, :], preferred_element_type=f32
        )


def attend(where, own, other):
    _, rows, width = own.shape
    return call(
        attend_body,
        "attend",
        where,
        (own, other),
        [whole(own.shape)] * 2,
        [jax.ShapeDtypeStruct((rows, width), bf16), jax.ShapeDtypeStruct((rows, width), f32)],
        flops=4 * rows * VIEW_ROWS * width,
    )


def renew_body(where, keep, got, old, steps, fresh):
    total = keep[...] + got[...].astype(f32)
    scale = lax.rsqrt(jnp.mean(total * total, axis=-1, keepdims=True) + epsilon)
    step = steps[where[5]]
    fresh[...] = (old[0].astype(f32) - step * (total * scale)).astype(bf16)


def renew(where, keep, got, weights, steps, group, groups):
    parts, rows, width = keep.shape
    return call(
        renew_body,
        "renew",
        where,
        (keep, got, weights, steps),
        [
            whole(keep.shape),
            whole(got.shape),
            pl.BlockSpec(
                (1, parts, rows, width), lambda i, w: (w[5], 0, w[6 + group], 0)
            ),
            pl.BlockSpec(memory_space=pltpu.SMEM),
        ],
        [jax.ShapeDtypeStruct(keep.shape, bf16)],
    )[0]


def finish_body(where, queries, attended, *refs):
    weights = refs[:8]
    outs, full = refs[8:-1], refs[-1]
    bit, is_owner = where[2], where[8]
    quarter = weights[0].shape[1]

    def place(blocks):
        for side in range(2):
            half = bit if side == 0 else 1 - bit
            for g in range(2):
                at = pl.ds(pl.multiple_of(half * 2 * quarter + g * quarter, quarter), quarter)
                for i in range(3):
                    full[i, at, :] = blocks[2 * side + g][i]

    @pl.when(is_owner == 1)
    def _():
        place(weights[:4])

    @pl.when(is_owner == 0)
    def _():
        place(weights[4:])

    for step, out in enumerate(outs):
        at = pl.ds(pl.multiple_of((where[0] ^ step) * VIEW_ROWS, VIEW_ROWS), VIEW_ROWS)
        q = queries[at, :]
        pre_gate = jnp.dot(q, full[0], preferred_element_type=f32)
        pre_up = jnp.dot(q, full[1], preferred_element_type=f32)
        hidden = (pre_gate * jax.nn.sigmoid(pre_gate) * pre_up).astype(bf16)
        fast = jnp.dot(hidden, full[2], preferred_element_type=f32)
        scale = lax.rsqrt(jnp.mean(fast * fast, axis=-1, keepdims=True) + epsilon)
        out[...] = (fast * scale + attended[at, :]).astype(bf16)


def finish(where, queries, attended, weights, heads):
    width = queries.shape[1]
    inputs = (queries, attended, *weights)
    return call(
        finish_body,
        "finish",
        where,
        inputs,
        [whole(x.shape) for x in inputs],
        [jax.ShapeDtypeStruct((VIEW_ROWS, width), bf16)] * heads,
        scratch=[pltpu.VMEM((3, width, width), bf16)],
        flops=6 * queries.shape[0] * width * width,
    )


def join_body(heads, width, where, *refs):
    out = refs[-1]
    for step in range(heads):
        head = head_of(where[0] ^ step, heads)
        out[:, pl.ds(pl.multiple_of(head * width, width), width)] = refs[step][...]


def join(where, blocks, heads, width):
    rows = blocks[0].shape[0]
    return call(
        functools.partial(join_body, heads, width),
        "join",
        where,
        tuple(blocks),
        [whole(x.shape) for x in blocks],
        [jax.ShapeDtypeStruct((rows, heads * width), bf16)],
    )[0]


def on_device(
    update_keys,
    update_values,
    update_rates,
    update_mask,
    fast_weights,
    step_sizes,
    target_queries,
    target_keys,
    target_values,
    target_views,
):
    heads, _, width, _ = fast_weights.shape
    half = heads // 2
    count = lax.axis_size(AXIS)
    me = lax.axis_index(AXIS)
    span = count // heads
    plane, inner = me // span, me % span
    core = inner % 2
    inner_bits = list(range(1, span.bit_length() - 1))
    bit_of = lambda b: (me >> b) & 1
    matched = lambda t: (t // span) % 2 == t % 2

    share = width // 4 // 2 ** (len(inner_bits) - 1)
    first = [bit_of(1) * 2 + g for g in range(2)]
    for b in inner_bits[1:]:
        first = [2 * f + bit_of(b) for f in first]
    is_owner = (plane % 2 == core).astype(i32)
    where = jnp.stack(
        [plane, core, bit_of(1), me, inner, head_of(plane, heads), first[0], first[1], is_owner]
    ).astype(i32)

    rates = -(update_mask.astype(f32)[:, None] * update_rates)
    tag = jnp.stack([target_views // 256, target_views % 256]).astype(bf16)
    tag = jnp.concatenate([tag, jnp.zeros((TAG_ROWS - 2, tag.shape[1]), bf16)])
    tag_in = swap(tag, 1)
    other = swap(pack_update(where, update_keys, update_values, rates, half, width), 1)
    tags = jnp.concatenate([tag[:2], tag_in[:2], jnp.zeros((TAG_ROWS - 4, tag.shape[1]), bf16)])

    sent = pack_target(where, target_queries, target_keys, target_values, tags, heads, width)
    pieces = {}
    for step in range(heads):
        group = {step * span: swap(sent[step], step * span) if step else sent[0]}
        for b in reversed(inner_bits):
            group.update({n | (1 << b): swap(x, 1 << b) for n, x in list(group.items())})
        pieces.update(group)
    own, given = arrange(
        where, [pieces[n] for n in sorted(pieces)], count, span, heads, width
    )
    queries, attended = attend(where, own, swap(given, 1))

    sums = []
    for j in range(half):
        sends, keeps = head_grad(
            where, update_keys, update_values, rates, other, fast_weights, j, half, width
        )
        for g in range(2):
            total = keeps[g] + swap(sends[g], 2).astype(f32)
            for b in inner_bits[1:]:
                rows = total.shape[1] // 2
                send = lax.dynamic_slice_in_dim(total, (1 - bit_of(b)) * rows, rows, 1)
                keep = lax.dynamic_slice_in_dim(total, bit_of(b) * rows, rows, 1)
                total = keep + swap(send.astype(bf16), 1 << b).astype(f32)
            total = total + swap(total.astype(bf16), span, lambda t: not matched(t)).astype(f32)
            sums.append(total)
    fresh = []
    upper = plane // 2 == 1
    for g in range(2):
        low, high = sums[g], sums[2 + g]
        keep = jnp.where(upper, high, low)
        got = swap(jnp.where(upper, low, high).astype(bf16), 2 * span, matched)
        new = renew(where, keep, got, fast_weights, step_sizes, g, 2)
        for b in reversed(inner_bits[1:]):
            far = swap(new, 1 << b, matched)
            new = jnp.where(
                bit_of(b) == 1,
                jnp.concatenate([far, new], axis=1),
                jnp.concatenate([new, far], axis=1),
            )
        fresh.append(new)
    far = [swap(x, 2, matched) for x in fresh]
    near = [swap(x, 1, matched) for x in fresh] + [swap(x, 1, matched) for x in far]

    blocks = finish(where, queries, attended, fresh + far + near, heads)
    got = [swap(x, step * span) if step else x for step, x in enumerate(blocks)]
    return join(where, got, heads, width)


def solution(mesh):
    rows = P(("groups", "tokens"), None)
    return jax.shard_map(
        on_device,
        mesh=mesh,
        in_specs=(
            rows,
            rows,
            rows,
            P(("groups", "tokens")),
            P(),
            P(),
            rows,
            rows,
            rows,
            P(("groups", "tokens")),
        ),
        out_specs=rows,
        check_vma=False,
    )
```

```python
import functools

import jax
import jax.numpy as jnp
from jax import lax
from jax.experimental import pallas as pl
from jax.experimental.pallas import tpu as pltpu
from jax.sharding import PartitionSpec as P

VIEW_ROWS = 128
AXIS = "tokens"
epsilon = 1e-05
f32 = jnp.float32
bf16 = jnp.bfloat16
i32 = jnp.int32
TAG_ROWS = 16
VMEM_LIMIT = 24 * 1024 * 1024


def swap(value, mask, senders=None):
    count = lax.axis_size(AXIS)
    pairs = [(t, t ^ mask) for t in range(count) if senders is None or senders(t)]
    return lax.ppermute(value, AXIS, pairs)


def after(value, *others):
    return lax.optimization_barrier((value, *others))[0]


def head_of(plane, head_count):
    half = head_count // 2
    return (plane % 2) * half + plane // 2


def whole(shape):
    return pl.BlockSpec(shape, lambda *_: (0,) * len(shape))


def call(body, name, scalars, inputs, specs, outs, grid=(1,), out_specs=None, scratch=()):
    return pl.pallas_call(
        body,
        name=name,
        grid_spec=pltpu.PrefetchScalarGridSpec(
            num_scalar_prefetch=1,
            grid=grid,
            in_specs=specs,
            out_specs=out_specs or [whole(o.shape) for o in outs],
            scratch_shapes=list(scratch),
        ),
        out_shape=list(outs),
        cost_estimate=pl.CostEstimate(flops=0, bytes_accessed=0, transcendentals=0),
        compiler_params=pltpu.CompilerParams(vmem_limit_bytes=VMEM_LIMIT),
    )(scalars, *inputs)


def rate_column(rates, mask, head):
    at = lax.broadcasted_iota(i32, rates.shape, 0) == head
    row = jnp.sum(jnp.where(at, rates, 0.0), axis=0, keepdims=True) * mask.astype(f32)
    return -jnp.transpose(jnp.broadcast_to(row, (8, row.shape[1])))[:, 0:1]


def pack_update_body(lane, half, where, rates, mask, keys, values, out, rows_s, tg_s, in_sem, out_sem):
    rows, width = rows_s.shape[1:]
    head = (1 - where[1]) * half + lane
    cols = pl.ds(pl.multiple_of(head * width, width), width)
    loads = []
    for i, source in ((1, values), (0, keys)):
        loads.append(pltpu.make_async_copy(source.at[:, cols], rows_s.at[i], in_sem.at[i]))
        loads[-1].start()
    rate = rate_column(rates[...], mask[...], head)
    loads[0].wait()
    tg_s[...] = (rate * rows_s[1].astype(f32)).astype(bf16)
    stores = [pltpu.make_async_copy(tg_s, out.at[1], out_sem.at[1])]
    stores[0].start()
    loads[1].wait()
    stores.append(pltpu.make_async_copy(rows_s.at[0], out.at[0], out_sem.at[0]))
    stores[1].start()
    for store in stores:
        store.wait()


def pack_update(where, rates, mask, keys, values, lane, half, width):
    rows = keys.shape[0]
    return call(
        functools.partial(pack_update_body, lane, half),
        "pack_update_%d" % lane,
        where,
        (rates, mask, keys, values),
        [whole(rates.shape), whole(mask.shape)] + [pl.BlockSpec(memory_space=pltpu.HBM)] * 2,
        [jax.ShapeDtypeStruct((2, rows, width), bf16)],
        out_specs=[pl.BlockSpec(memory_space=pl.ANY)],
        scratch=[
            pltpu.VMEM((2, rows, width), bf16),
            pltpu.VMEM((rows, width), bf16),
            pltpu.SemaphoreType.DMA((2,)),
            pltpu.SemaphoreType.DMA((2,)),
        ],
    )[0]


def pack_target_body(heads, width, where, queries, keys, values, views, *outs):
    rows = queries.shape[0]
    for step in range(heads):
        head = head_of(where[0] ^ step, heads)
        cols = pl.ds(pl.multiple_of(head * width, width), width)
        for i, source in enumerate((queries, keys, values)):
            outs[step][pl.ds(i * rows, rows), :] = source[:, cols]
        outs[step][pl.ds(3 * rows, TAG_ROWS), :] = jnp.zeros((TAG_ROWS, width), bf16)
        high, low = views[...] // 256, views[...] % 256
        row_at = lax.broadcasted_iota(i32, (TAG_ROWS, rows), 0)
        digits = jnp.where(row_at == 0, high, jnp.where(row_at == 1, low, 0))
        outs[step][pl.ds(3 * rows, TAG_ROWS), pl.ds(0, rows)] = digits.astype(f32).astype(bf16)


def pack_target(where, queries, keys, values, views, heads, width):
    rows = queries.shape[0]
    out = jax.ShapeDtypeStruct((3 * rows + TAG_ROWS, width), bf16)
    inputs = (queries, keys, values, views)
    return call(
        functools.partial(pack_target_body, heads, width),
        "pack_target",
        where,
        inputs,
        [whole(x.shape) for x in inputs],
        [out] * heads,
    )


def head_grad_body(
    lane, half, cut, where, rates, mask, keys, values, other, weights, *refs
):
    sends, keeps = refs[:2], refs[2:4]
    k_s, v_s, w_s, tg_s, hidden_s, gate_s, up_s, full, send_s, keep_s, in_sem, out_sem = refs[4:]
    rows, width = v_s.shape
    head = where[1] * half + lane
    cols = pl.ds(pl.multiple_of(head * width, width), width)
    upper, lower = pl.ds(0, rows), pl.ds(rows, rows)
    loads = [
        pltpu.make_async_copy(keys.at[:, cols], k_s.at[upper], in_sem.at[0]),
        pltpu.make_async_copy(weights.at[head, 0], w_s.at[0], in_sem.at[1]),
        pltpu.make_async_copy(weights.at[head, 1], w_s.at[1], in_sem.at[2]),
        pltpu.make_async_copy(values.at[:, cols], v_s, in_sem.at[3]),
        pltpu.make_async_copy(weights.at[head, 2], w_s.at[2], in_sem.at[4]),
        pltpu.make_async_copy(other.at[0], k_s.at[lower], in_sem.at[5]),
        pltpu.make_async_copy(other.at[1], tg_s.at[lower], in_sem.at[6]),
    ]
    for load in loads:
        load.start()
    rate = rate_column(rates[...], mask[...], head)
    chunk = 256
    for at in range(0, 2 * rows, chunk):
        span = pl.ds(at, chunk)
        if at == 0:
            loads[0].wait()
            loads[1].wait()
        if at == rows:
            loads[5].wait()
        k = k_s[span, :]
        pre_gate = jnp.dot(k, w_s[0], preferred_element_type=f32)
        if at == 0:
            loads[2].wait()
        pre_up = jnp.dot(k, w_s[1], preferred_element_type=f32)
        if at == 0:
            loads[3].wait()
            loads[4].wait()
        if at == rows:
            loads[6].wait()
        if at < rows:
            tg = (rate[at : at + chunk] * v_s[span, :].astype(f32)).astype(bf16)
            tg_s[span, :] = tg
        else:
            tg = tg_s[span, :]
        back = lax.dot_general(tg, w_s[2], (((1,), (1,)), ((), ())), preferred_element_type=f32)
        sigma = 0.5 * jnp.tanh(0.5 * pre_gate) + 0.5
        activated = pre_gate * sigma
        hidden_s[span, :] = (activated * pre_up).astype(bf16)
        gate_s[span, :] = (back * pre_up * (sigma + activated * (1.0 - sigma))).astype(bf16)
        up_s[span, :] = (back * activated).astype(bf16)
    quarter = width // 4
    bit = where[2]
    stores = []
    for i, left, right in ((2, hidden_s, tg_s), (0, k_s, gate_s), (1, k_s, up_s)):
        full[...] = lax.dot_general(
            left[...], right[...], (((0,), (0,)), ((), ())), preferred_element_type=f32
        )
        for g in range(2):
            for side in range(2):
                at = pl.ds((2 * side + g) * quarter, quarter)
                if cut:
                    rows_at = pl.ds(
                        pl.multiple_of(((bit + 1 - side) % 2) * 2 * quarter + g * quarter, quarter),
                        quarter,
                    )
                    if side == 0:
                        send_s[g, i] = full[rows_at, :].astype(bf16)
                    else:
                        keep_s[g, i] = full[rows_at, :]
                else:
                    half_at = pl.ds(side * quarter, quarter)
                    send_s[g, i, half_at] = full[at, :].astype(bf16)
                    keep_s[g, i, half_at] = full[at, :]
            stores += [
                (pltpu.make_async_copy(send_s.at[g, i], sends[g].at[i], out_sem.at[0, g, i]), 0),
                (pltpu.make_async_copy(keep_s.at[g, i], keeps[g].at[i], out_sem.at[1, g, i]), 1),
            ]
            for store, when in stores[-2:]:
                if cut:
                    store.start()
                else:
                    pl.when(where[8] == when)(store.start)
    for store, when in stores:
        if cut:
            store.wait()
        else:
            pl.when(where[8] == when)(store.wait)


def head_grad(where, rates, mask, keys, values, other, weights, lane, half, width, cut):
    rows = keys.shape[0]
    shape = (3, width // 4 if cut else width // 2, width)
    anywhere = pl.BlockSpec(memory_space=pl.ANY)
    in_hbm = pl.BlockSpec(memory_space=pltpu.HBM)
    both = pltpu.VMEM((2 * rows, width), bf16)
    outs = call(
        functools.partial(head_grad_body, lane, half, cut),
        "head_grad_%d" % lane,
        where,
        (rates, mask, keys, values, other, weights),
        [whole(rates.shape), whole(mask.shape), in_hbm, in_hbm, anywhere, in_hbm],
        [jax.ShapeDtypeStruct(shape, bf16)] * 2 + [jax.ShapeDtypeStruct(shape, f32)] * 2,
        out_specs=[anywhere] * 4,
        scratch=[
            both,
            pltpu.VMEM((rows, width), bf16),
            pltpu.VMEM((3, width, width), bf16),
            both,
            both,
            both,
            both,
            pltpu.VMEM((width, width), f32),
            pltpu.VMEM((2, *shape), bf16),
            pltpu.VMEM((2, *shape), f32),
            pltpu.SemaphoreType.DMA((7,)),
            pltpu.SemaphoreType.DMA((2, 2, 3)),
        ],
    )
    return outs[:2], outs[2:]


def arrange_body(span, where, *refs):
    pieces, out = refs[:-1], refs[-1]
    me, inner = where[3], where[4]
    rows = (pieces[0].shape[0] - TAG_ROWS) // 3
    count = len(pieces)
    heads = count // span
    tags = [p[pl.ds(3 * rows, TAG_ROWS), pl.ds(0, rows)].astype(f32) for p in pieces]
    ids = jnp.concatenate([t[0:1, :] * 256.0 + t[1:2, :] for t in tags], axis=0).astype(i32)
    square = (count, count)
    earlier = (
        (me ^ lax.broadcasted_iota(i32, square, 1)) < (me ^ lax.broadcasted_iota(i32, square, 0))
    ).astype(f32)
    before = (
        lax.broadcasted_iota(i32, (rows, rows), 0) < lax.broadcasted_iota(i32, (rows, rows), 1)
    ).astype(f32)
    place = jnp.full((count, rows), -1.0, f32)
    for j in range(heads):
        hit = (ids == j * span + inner).astype(f32)
        rank = jnp.dot(hit, before, preferred_element_type=f32) + jnp.sum(
            jnp.dot(earlier, hit, preferred_element_type=f32), axis=1, keepdims=True
        )
        place = jnp.where(hit > 0.0, rank + float(j * VIEW_ROWS), place)
    place = place.astype(i32)
    group = 4
    totals = [None] * 3
    for first in range(0, count, group):
        row_at = lax.broadcasted_iota(i32, (heads * VIEW_ROWS, rows), 0)
        pick = jnp.concatenate(
            [
                (row_at == place[n : n + 1, :]).astype(f32).astype(bf16)
                for n in range(first, first + group)
            ],
            axis=1,
        )
        for i in range(3):
            source = jnp.concatenate(
                [pieces[n][pl.ds(i * rows, rows), :] for n in range(first, first + group)],
                axis=0,
            )
            part = jnp.dot(pick, source, preferred_element_type=f32)
            totals[i] = part if totals[i] is None else totals[i] + part
    for i in range(3):
        out[i] = totals[i].astype(bf16)


def arrange(where, pieces, span, heads, width):
    return call(
        functools.partial(arrange_body, span),
        "arrange",
        where,
        tuple(pieces),
        [whole(x.shape) for x in pieces],
        [jax.ShapeDtypeStruct((3, heads * VIEW_ROWS, width), bf16)],
    )[0]


def attend_body(where, rows, attended):
    width = rows.shape[2]
    for v in range(rows.shape[1] // VIEW_ROWS):
        at = pl.ds(v * VIEW_ROWS, VIEW_ROWS)
        scores = lax.dot_general(
            rows[0, at, :], rows[1, at, :], (((1,), (1,)), ((), ())), preferred_element_type=f32
        ) * width ** (-0.5)
        top = jnp.max(scores, axis=1, keepdims=True)
        raised = jnp.exp(scores - top)
        probs = (raised / jnp.sum(raised, axis=1, keepdims=True)).astype(bf16)
        attended[at, :] = jnp.dot(probs, rows[2, at, :], preferred_element_type=f32)


def attend(where, rows):
    return call(
        attend_body,
        "attend",
        where,
        (rows,),
        [whole(rows.shape)],
        [jax.ShapeDtypeStruct(rows.shape[1:], f32)],
    )[0]


def renew_body(where, keep, got, old, steps, fresh):
    total = keep[...] + got[...].astype(f32)
    scale = lax.rsqrt(jnp.mean(total * total, axis=-1, keepdims=True) + epsilon)
    step = steps[where[5]]
    fresh[...] = (old[0].astype(f32) - step * (total * scale)).astype(bf16)


def renew(where, keep, got, weights, steps, group, groups):
    parts, rows, width = keep.shape
    return call(
        renew_body,
        "renew",
        where,
        (keep, got, weights, steps),
        [
            whole(keep.shape),
            whole(got.shape),
            pl.BlockSpec(
                (1, parts, rows, width), lambda i, w: (w[5], 0, w[6 + group], 0)
            ),
            pl.BlockSpec(memory_space=pltpu.SMEM),
        ],
        [jax.ShapeDtypeStruct(keep.shape, bf16)],
    )[0]


def finish_body(where, rows, attended, *refs):
    weights = refs[:8]
    outs, full = refs[8:-1], refs[-1]
    bit, is_owner = where[2], where[8]
    quarter = weights[0].shape[1]

    def place(blocks):
        for side in range(2):
            half = bit if side == 0 else 1 - bit
            for g in range(2):
                at = pl.ds(pl.multiple_of(half * 2 * quarter + g * quarter, quarter), quarter)
                for i in range(3):
                    full[i, at, :] = blocks[2 * side + g][i]

    @pl.when(is_owner == 1)
    def _():
        place(weights[:4])

    @pl.when(is_owner == 0)
    def _():
        place(weights[4:])

    for step, out in enumerate(outs):
        at = pl.ds(pl.multiple_of((where[0] ^ step) * VIEW_ROWS, VIEW_ROWS), VIEW_ROWS)
        q = rows[0, at, :]
        pre_gate = jnp.dot(q, full[0], preferred_element_type=f32)
        pre_up = jnp.dot(q, full[1], preferred_element_type=f32)
        hidden = (pre_gate * jax.nn.sigmoid(pre_gate) * pre_up).astype(bf16)
        fast = jnp.dot(hidden, full[2], preferred_element_type=f32)
        scale = lax.rsqrt(jnp.mean(fast * fast, axis=-1, keepdims=True) + epsilon)
        out[...] = (fast * scale + attended[at, :]).astype(bf16)


def finish(where, rows, attended, weights, heads):
    width = rows.shape[2]
    inputs = (rows, attended, *weights)
    return call(
        finish_body,
        "finish",
        where,
        inputs,
        [pl.BlockSpec((1, *rows.shape[1:]), lambda i, w: (0, 0, 0))]
        + [whole(x.shape) for x in inputs[1:]],
        [jax.ShapeDtypeStruct((VIEW_ROWS, width), bf16)] * heads,
        scratch=[pltpu.VMEM((3, width, width), bf16)],
    )


def join_body(heads, width, where, *refs):
    out = refs[-1]
    for step in range(heads):
        head = head_of(where[0] ^ step, heads)
        out[:, pl.ds(pl.multiple_of(head * width, width), width)] = refs[step][...]


def join(where, blocks, heads, width):
    rows = blocks[0].shape[0]
    return call(
        functools.partial(join_body, heads, width),
        "join",
        where,
        tuple(blocks),
        [whole(x.shape) for x in blocks],
        [jax.ShapeDtypeStruct((rows, heads * width), bf16)],
    )[0]


def on_device(
    update_keys,
    update_values,
    update_rates,
    update_mask,
    fast_weights,
    step_sizes,
    target_queries,
    target_keys,
    target_values,
    target_views,
):
    heads, _, width, _ = fast_weights.shape
    half = heads // 2
    count = lax.axis_size(AXIS)
    me = lax.axis_index(AXIS)
    span = count // heads
    plane, inner = me // span, me % span
    core = inner % 2
    inner_bits = list(range(1, span.bit_length() - 1))
    bit_of = lambda b: (me >> b) & 1
    matched = lambda t: (t // span) % 2 == t % 2

    share = width // 4 // 2 ** (len(inner_bits) - 1)
    first = [bit_of(1) * 2 + g for g in range(2)]
    for b in inner_bits[1:]:
        first = [2 * f + bit_of(b) for f in first]
    is_owner = (plane % 2 == core).astype(i32)
    where = jnp.stack(
        [plane, core, bit_of(1), me, inner, head_of(plane, heads), first[0], first[1], is_owner]
    ).astype(i32)

    rates, mask = update_rates.T, update_mask[None, :]

    turn = where

    others = []
    for j in range(half):
        packed = pack_update(turn, rates, mask, update_keys, update_values, j, half, width)
        turn = after(turn, packed)
        others.append(swap(packed, 1))
        if j == 0:
            sent = pack_target(
                turn, target_queries, target_keys, target_values, target_views[None, :], heads, width
            )
            turn = after(turn, sent[0])

    group = {0: sent[0]}
    came = {step: swap(sent[step], step * span) for step in (1, 2)}

    def spread(step, bits):
        for b in bits:
            for n, x in list(group.items()):
                if n // span == step:
                    group[n | (1 << b)] = swap(x, 1 << b)

    outer_bits = list(reversed(inner_bits))
    spread(0, outer_bits)

    sends, keeps = head_grad(
        turn, rates, mask, update_keys, update_values, others[0], fast_weights, 0, half, width, True
    )
    moved = [swap(x, 2) for x in sends]
    turn = after(turn, sends[0], came[1], *group.values())
    spread(0, [0])
    group[span] = came[1]
    whole_sends, whole_keeps = head_grad(
        turn, rates, mask, update_keys, update_values, others[1], fast_weights, 1, half, width, False
    )
    crossed = [swap(x, span, lambda t: not matched(t)) for x in whole_sends]
    turn = after(turn, whole_sends[0])

    def narrow(total, bits, senders=None):
        for b in bits:
            rows = total.shape[1] // 2
            send = lax.dynamic_slice_in_dim(total, (1 - bit_of(b)) * rows, rows, 1)
            keep = lax.dynamic_slice_in_dim(total, bit_of(b) * rows, rows, 1)
            total = keep + swap(send.astype(bf16), 1 << b, senders).astype(f32)
        return total

    low = []
    for g in range(2):
        total = after(keeps[g], turn) + moved[g].astype(f32)
        total = narrow(total, inner_bits[1:])
        low.append((total, swap(total.astype(bf16), span, lambda t: not matched(t))))
        turn = after(turn, total)
        if g == 0:
            turn = after(turn, came[2])
            group[2 * span] = came[2]
            came[3] = swap(after(sent[3], turn), 3 * span)
    group[span] = after(group[span], turn)
    spread(1, outer_bits)
    high = []
    for g in range(2):
        total = after(whole_keeps[g], turn) + crossed[g].astype(f32)
        turn = after(turn, total)
        high.append(narrow(total, inner_bits, matched))
    group[2 * span] = after(group[2 * span], turn)
    spread(2, outer_bits)
    turn = after(turn, *[x for n, x in group.items() if n // span == 0])

    fresh = []
    upper = plane // 2 == 1
    for g in range(2):
        mine_low = after(low[g][0], turn) + low[g][1].astype(f32)
        keep = jnp.where(upper, high[g], mine_low)
        got = swap(jnp.where(upper, mine_low, high[g]).astype(bf16), 2 * span, matched)
        turn = after(turn, keep)
        if g == 0:
            turn = after(turn, came[3])
            group[3 * span] = came[3]
            spread(3, outer_bits)
            spread(1, [0])
        new = renew(turn, keep, got, fast_weights, step_sizes, g, 2)
        turn = after(turn, new)
        for b in reversed(inner_bits[1:]):
            far = swap(new, 1 << b, matched)
            new = jnp.where(
                bit_of(b) == 1,
                jnp.concatenate([far, new], axis=1),
                jnp.concatenate([new, far], axis=1),
            )
        fresh.append(new)
    spread(2, [0])
    spread(3, [0])
    far = [swap(x, 2, matched) for x in fresh]
    near = [swap(x, 1, matched) for x in fresh] + [swap(x, 1, matched) for x in far]

    rows = arrange(turn, [group[n] for n in sorted(group)], span, heads, width)
    attended = attend(turn, rows)
    blocks = finish(where, rows, attended, fresh + far + near, heads)
    got = [swap(x, step * span) if step else x for step, x in enumerate(blocks)]
    return join(where, got, heads, width)


def solution(mesh):
    rows = P(("groups", "tokens"), None)
    return jax.shard_map(
        on_device,
        mesh=mesh,
        in_specs=(
            rows,
            rows,
            rows,
            P(("groups", "tokens")),
            P(),
            P(),
            rows,
            rows,
            rows,
            P(("groups", "tokens")),
        ),
        out_specs=rows,
        check_vma=False,
    )
```

```python
import functools

import jax
import jax.numpy as jnp
from jax import lax
from jax.experimental import pallas as pl
from jax.experimental.pallas import tpu as pltpu
from jax.sharding import PartitionSpec as P

VIEW_ROWS = 128
AXIS = "tokens"
epsilon = 1e-05
f32 = jnp.float32
bf16 = jnp.bfloat16
i32 = jnp.int32
TAG_ROWS = 16
MIB = 1024 * 1024


def swap(value, mask, senders=None):
    count = lax.axis_size(AXIS)
    pairs = [(t, t ^ mask) for t in range(count) if senders is None or senders(t)]
    return lax.ppermute(value, AXIS, pairs)


def after(value, *others):
    return lax.optimization_barrier((value, *others))[0]


def head_of(plane, head_count):
    half = head_count // 2
    return (plane % 2) * half + plane // 2


def whole(shape):
    return pl.BlockSpec(shape, lambda *_: (0,) * len(shape))


def call(body, name, scalars, inputs, specs, outs, grid=(1,), out_specs=None, scratch=(), vmem=8):
    return pl.pallas_call(
        body,
        name=name,
        grid_spec=pltpu.PrefetchScalarGridSpec(
            num_scalar_prefetch=1,
            grid=grid,
            in_specs=specs,
            out_specs=out_specs or [whole(o.shape) for o in outs],
            scratch_shapes=list(scratch),
        ),
        out_shape=list(outs),
        cost_estimate=pl.CostEstimate(flops=0, bytes_accessed=0, transcendentals=0),
        compiler_params=pltpu.CompilerParams(vmem_limit_bytes=vmem * MIB),
    )(scalars, *inputs)


def rate_column(rates, mask, head):
    at = lax.broadcasted_iota(i32, rates.shape, 0) == head
    row = jnp.sum(jnp.where(at, rates, 0.0), axis=0, keepdims=True) * mask.astype(f32)
    return -jnp.transpose(jnp.broadcast_to(row, (8, row.shape[1])))[:, 0:1]


def pack_body(heads, where, rates, mask, views, keys, values, *refs):
    half = heads // 2
    target, refs = refs[:3], refs[3:]
    packed, sent = refs[:half], refs[half : half + heads]
    value_s, pack_s, sent_s, in_sem, target_sem, out_sem = refs[half + heads :]
    rows, width = value_s.shape[1:]
    count = target[0].shape[0]

    def columns(head):
        return pl.ds(pl.multiple_of(head * width, width), width)

    loads = []
    for j in range(half):
        head = (1 - where[1]) * half + j
        for i, to in ((1, value_s.at[j]), (0, pack_s.at[j, 0])):
            source = (keys, values)[i]
            loads.append(pltpu.make_async_copy(source.at[:, columns(head)], to, in_sem.at[j, i]))
            loads[-1].start()
    rows_in = []
    for step in range(heads):
        head = head_of(where[0] ^ step, heads)
        for i in range(3):
            to = sent_s.at[step, pl.ds(i * count, count)]
            rows_in.append(
                pltpu.make_async_copy(
                    target[i].at[:, columns(head)], to, target_sem.at[step, i]
                )
            )
            rows_in[-1].start()
    row_at = lax.broadcasted_iota(i32, (TAG_ROWS, count), 0)
    digits = jnp.where(
        row_at == 0, views[...] // 256, jnp.where(row_at == 1, views[...] % 256, 0)
    )
    for step in range(heads):
        sent_s[step, pl.ds(3 * count, TAG_ROWS), :] = jnp.zeros((TAG_ROWS, width), bf16)
        sent_s[step, pl.ds(3 * count, TAG_ROWS), pl.ds(0, count)] = digits.astype(f32).astype(bf16)
    stores = []
    for j in range(half):
        rate = rate_column(rates[...], mask[...], (1 - where[1]) * half + j)
        loads[2 * j].wait()
        pack_s[j, 1] = (rate * value_s[j].astype(f32)).astype(bf16)
        loads[2 * j + 1].wait()
        stores.append(pltpu.make_async_copy(pack_s.at[j], packed[j], out_sem.at[j]))
        stores[-1].start()
    for step in range(heads):
        for i in range(3):
            rows_in[3 * step + i].wait()
        stores.append(pltpu.make_async_copy(sent_s.at[step], sent[step], out_sem.at[half + step]))
        stores[-1].start()
    for store in stores:
        store.wait()


def pack(where, rates, mask, views, keys, values, target, heads, width):
    half, rows, count = heads // 2, keys.shape[0], views.shape[1]
    small = (rates, mask, views)
    anywhere = pl.BlockSpec(memory_space=pl.ANY)
    piece = (3 * count + TAG_ROWS, width)
    outs = call(
        functools.partial(pack_body, heads),
        "pack",
        where,
        (*small, keys, values, *target),
        [whole(x.shape) for x in small] + [anywhere] * 5,
        [jax.ShapeDtypeStruct((2, rows, width), bf16)] * half
        + [jax.ShapeDtypeStruct(piece, bf16)] * heads,
        out_specs=[anywhere] * (half + heads),
        scratch=[
            pltpu.VMEM((half, rows, width), bf16),
            pltpu.VMEM((half, 2, rows, width), bf16),
            pltpu.VMEM((heads, *piece), bf16),
            pltpu.SemaphoreType.DMA((half, 2)),
            pltpu.SemaphoreType.DMA((heads, 3)),
            pltpu.SemaphoreType.DMA((half + heads,)),
        ],
        vmem=62,
    )
    return outs[:half], outs[half:]


def head_grad_body(
    lane, half, where, rates, mask, keys, values, other, weights, *refs
):
    sends, keeps = refs[:2], refs[2:4]
    k_s, v_s, w_s, tg_s, hidden_s, gate_s, up_s, full, send_s, keep_s, in_sem, out_sem = refs[4:]
    rows, width = v_s.shape
    head = where[1] * half + lane
    cols = pl.ds(pl.multiple_of(head * width, width), width)
    upper, lower = pl.ds(0, rows), pl.ds(rows, rows)
    loads = [
        pltpu.make_async_copy(keys.at[:, cols], k_s.at[upper], in_sem.at[0]),
        pltpu.make_async_copy(weights.at[head, 0], w_s.at[0], in_sem.at[1]),
        pltpu.make_async_copy(weights.at[head, 1], w_s.at[1], in_sem.at[2]),
        pltpu.make_async_copy(values.at[:, cols], v_s, in_sem.at[3]),
        pltpu.make_async_copy(weights.at[head, 2], w_s.at[2], in_sem.at[4]),
        pltpu.make_async_copy(other.at[0], k_s.at[lower], in_sem.at[5]),
        pltpu.make_async_copy(other.at[1], tg_s.at[lower], in_sem.at[6]),
    ]
    for load in loads:
        load.start()
    rate = rate_column(rates[...], mask[...], head)
    chunk = 256
    for at in range(0, 2 * rows, chunk):
        span = pl.ds(at, chunk)
        if at == 0:
            loads[0].wait()
            loads[1].wait()
        if at == rows:
            loads[5].wait()
        k = k_s[span, :]
        pre_gate = jnp.dot(k, w_s[0], preferred_element_type=f32)
        if at == 0:
            loads[2].wait()
        pre_up = jnp.dot(k, w_s[1], preferred_element_type=f32)
        if at == 0:
            loads[3].wait()
            loads[4].wait()
        if at == rows:
            loads[6].wait()
        if at < rows:
            tg = (rate[at : at + chunk] * v_s[span, :].astype(f32)).astype(bf16)
            tg_s[span, :] = tg
        else:
            tg = tg_s[span, :]
        back = lax.dot_general(tg, w_s[2], (((1,), (1,)), ((), ())), preferred_element_type=f32)
        sigma = 0.5 * jnp.tanh(0.5 * pre_gate) + 0.5
        activated = pre_gate * sigma
        hidden_s[span, :] = (activated * pre_up).astype(bf16)
        gate_s[span, :] = (back * pre_up * (sigma + activated * (1.0 - sigma))).astype(bf16)
        up_s[span, :] = (back * activated).astype(bf16)
    quarter = width // 4
    bit = where[2]
    stores = []
    for i, left, right in ((2, hidden_s, tg_s), (0, k_s, gate_s), (1, k_s, up_s)):
        full[...] = lax.dot_general(
            left[...], right[...], (((0,), (0,)), ((), ())), preferred_element_type=f32
        )
        for g in range(2):
            kept = pl.ds(pl.multiple_of(bit * 2 * quarter + g * quarter, quarter), quarter)
            sent = pl.ds(pl.multiple_of((1 - bit) * 2 * quarter + g * quarter, quarter), quarter)
            send_s[g, i] = full[sent, :].astype(bf16)
            keep_s[g, i] = full[kept, :]
            stores += [
                pltpu.make_async_copy(send_s.at[g, i], sends[g].at[i], out_sem.at[0, g, i]),
                pltpu.make_async_copy(keep_s.at[g, i], keeps[g].at[i], out_sem.at[1, g, i]),
            ]
            stores[-2].start()
            stores[-1].start()
    for store in stores:
        store.wait()


def head_grad(where, rates, mask, keys, values, other, weights, lane, half, width):
    rows = keys.shape[0]
    shape = (3, width // 4, width)
    anywhere = pl.BlockSpec(memory_space=pl.ANY)
    in_hbm = pl.BlockSpec(memory_space=pltpu.HBM)
    both = pltpu.VMEM((2 * rows, width), bf16)
    outs = call(
        functools.partial(head_grad_body, lane, half),
        "head_grad_%d" % lane,
        where,
        (rates, mask, keys, values, other, weights),
        [whole(rates.shape), whole(mask.shape), in_hbm, in_hbm, anywhere, in_hbm],
        [jax.ShapeDtypeStruct(shape, bf16)] * 2 + [jax.ShapeDtypeStruct(shape, f32)] * 2,
        out_specs=[anywhere] * 4,
        scratch=[
            both,
            pltpu.VMEM((rows, width), bf16),
            pltpu.VMEM((3, width, width), bf16),
            both,
            both,
            both,
            both,
            pltpu.VMEM((width, width), f32),
            pltpu.VMEM((2, *shape), bf16),
            pltpu.VMEM((2, *shape), f32),
            pltpu.SemaphoreType.DMA((7,)),
            pltpu.SemaphoreType.DMA((2, 2, 3)),
        ],
        vmem=62,
    )
    return outs[:2], outs[2:]


def arrange_body(slots, span, where, *refs):
    out = refs[-1]
    pieces = []
    for n, at in slots:
        pieces.append(refs[n] if at is None else refs[n].at[at])
    me, inner = where[3], where[4]
    rows = (pieces[0].shape[0] - TAG_ROWS) // 3
    count = len(pieces)
    heads = count // span
    tags = [p[pl.ds(3 * rows, TAG_ROWS), pl.ds(0, rows)].astype(f32) for p in pieces]
    ids = jnp.concatenate([t[0:1, :] * 256.0 + t[1:2, :] for t in tags], axis=0).astype(i32)
    square = (count, count)
    earlier = (
        (me ^ lax.broadcasted_iota(i32, square, 1)) < (me ^ lax.broadcasted_iota(i32, square, 0))
    ).astype(f32)
    before = (
        lax.broadcasted_iota(i32, (rows, rows), 0) < lax.broadcasted_iota(i32, (rows, rows), 1)
    ).astype(f32)
    place = jnp.full((count, rows), -1.0, f32)
    for j in range(heads):
        hit = (ids == j * span + inner).astype(f32)
        rank = jnp.dot(hit, before, preferred_element_type=f32) + jnp.sum(
            jnp.dot(earlier, hit, preferred_element_type=f32), axis=1, keepdims=True
        )
        place = jnp.where(hit > 0.0, rank + float(j * VIEW_ROWS), place)
    place = place.astype(i32)
    group = 4
    totals = [None] * 3
    for first in range(0, count, group):
        row_at = lax.broadcasted_iota(i32, (heads * VIEW_ROWS, rows), 0)
        pick = jnp.concatenate(
            [
                (row_at == place[n : n + 1, :]).astype(f32).astype(bf16)
                for n in range(first, first + group)
            ],
            axis=1,
        )
        for i in range(3):
            source = jnp.concatenate(
                [pieces[n][pl.ds(i * rows, rows), :] for n in range(first, first + group)],
                axis=0,
            )
            part = jnp.dot(pick, source, preferred_element_type=f32)
            totals[i] = part if totals[i] is None else totals[i] + part
    for i in range(3):
        out[i] = totals[i].astype(bf16)


def arrange(where, pieces, slots, span, heads, width):
    return call(
        functools.partial(arrange_body, slots, span),
        "arrange",
        where,
        tuple(pieces),
        [whole(x.shape) for x in pieces],
        [jax.ShapeDtypeStruct((3, heads * VIEW_ROWS, width), bf16)],
        vmem=20,
    )[0]


def attend_body(where, rows, attended):
    width = rows.shape[2]
    for v in range(rows.shape[1] // VIEW_ROWS):
        at = pl.ds(v * VIEW_ROWS, VIEW_ROWS)
        scores = lax.dot_general(
            rows[0, at, :], rows[1, at, :], (((1,), (1,)), ((), ())), preferred_element_type=f32
        ) * width ** (-0.5)
        top = jnp.max(scores, axis=1, keepdims=True)
        raised = jnp.exp(scores - top)
        probs = (raised / jnp.sum(raised, axis=1, keepdims=True)).astype(bf16)
        attended[at, :] = jnp.dot(probs, rows[2, at, :], preferred_element_type=f32)


def attend(where, rows):
    return call(
        attend_body,
        "attend",
        where,
        (rows,),
        [whole(rows.shape)],
        [jax.ShapeDtypeStruct(rows.shape[1:], f32)],
    )[0]


def renew_body(where, keep, got, old, steps, fresh):
    total = keep[...] + got[...].astype(f32)
    scale = lax.rsqrt(jnp.mean(total * total, axis=-1, keepdims=True) + epsilon)
    step = steps[where[5]]
    fresh[...] = (old[...].astype(f32) - step * (total * scale)).astype(bf16)


def renew(where, keep, got, old, steps):
    return call(
        renew_body,
        "renew",
        where,
        (keep, got, old, steps),
        [whole(keep.shape)] * 3 + [pl.BlockSpec(memory_space=pltpu.SMEM)],
        [jax.ShapeDtypeStruct(keep.shape, bf16)],
    )[0]


def finish_body(where, rows, attended, *refs):
    weights = refs[:8]
    outs, full = refs[8:-1], refs[-1]
    bit, is_owner = where[2], where[8]
    quarter = weights[0].shape[1]

    def place(blocks):
        for side in range(2):
            half = bit if side == 0 else 1 - bit
            for g in range(2):
                at = pl.ds(pl.multiple_of(half * 2 * quarter + g * quarter, quarter), quarter)
                for i in range(3):
                    full[i, at, :] = blocks[2 * side + g][i]

    @pl.when(is_owner == 1)
    def _():
        place(weights[:4])

    @pl.when(is_owner == 0)
    def _():
        place(weights[4:])

    for step, out in enumerate(outs):
        at = pl.ds(pl.multiple_of((where[0] ^ step) * VIEW_ROWS, VIEW_ROWS), VIEW_ROWS)
        q = rows[0, at, :]
        pre_gate = jnp.dot(q, full[0], preferred_element_type=f32)
        pre_up = jnp.dot(q, full[1], preferred_element_type=f32)
        hidden = (pre_gate * jax.nn.sigmoid(pre_gate) * pre_up).astype(bf16)
        fast = jnp.dot(hidden, full[2], preferred_element_type=f32)
        scale = lax.rsqrt(jnp.mean(fast * fast, axis=-1, keepdims=True) + epsilon)
        out[...] = (fast * scale + attended[at, :]).astype(bf16)


def finish(where, rows, attended, weights, heads):
    width = rows.shape[2]
    inputs = (rows, attended, *weights)
    return call(
        finish_body,
        "finish",
        where,
        inputs,
        [pl.BlockSpec((1, *rows.shape[1:]), lambda i, w: (0, 0, 0))]
        + [whole(x.shape) for x in inputs[1:]],
        [jax.ShapeDtypeStruct((VIEW_ROWS, width), bf16)] * heads,
        scratch=[pltpu.VMEM((3, width, width), bf16)],
        vmem=12,
    )


def join_body(heads, width, where, *refs):
    out = refs[-1]
    for step in range(heads):
        head = head_of(where[0] ^ step, heads)
        out[:, pl.ds(pl.multiple_of(head * width, width), width)] = refs[step][...]


def join(where, blocks, heads, width):
    rows = blocks[0].shape[0]
    return call(
        functools.partial(join_body, heads, width),
        "join",
        where,
        tuple(blocks),
        [whole(x.shape) for x in blocks],
        [jax.ShapeDtypeStruct((rows, heads * width), bf16)],
    )[0]


def on_device(
    update_keys,
    update_values,
    update_rates,
    update_mask,
    fast_weights,
    step_sizes,
    target_queries,
    target_keys,
    target_values,
    target_views,
):
    heads, _, width, _ = fast_weights.shape
    half = heads // 2
    count = lax.axis_size(AXIS)
    me = lax.axis_index(AXIS)
    span = count // heads
    plane, inner = me // span, me % span
    core = inner % 2
    inner_bits = list(range(1, span.bit_length() - 1))
    bit_of = lambda b: (me >> b) & 1
    matched = lambda t: (t // span) % 2 == t % 2

    share = width // 4 // 2 ** (len(inner_bits) - 1)
    first = [bit_of(1) * 2 + g for g in range(2)]
    for b in inner_bits[1:]:
        first = [2 * f + bit_of(b) for f in first]
    is_owner = (plane % 2 == core).astype(i32)
    where = jnp.stack(
        [plane, core, bit_of(1), me, inner, head_of(plane, heads), first[0], first[1], is_owner]
    ).astype(i32)

    rates, mask = update_rates.T, update_mask[None, :]

    turn = where

    others, sent = pack(
        turn,
        rates,
        mask,
        target_views[None, :],
        update_keys,
        update_values,
        (target_queries, target_keys, target_values),
        heads,
        width,
    )
    turn = after(turn, sent[0])
    others = [swap(x, 1) for x in others]

    outer_bits = list(reversed(inner_bits))

    def spread(parts, bits):
        for b in bits:
            parts.update({n | (1 << b): swap(x, 1 << b) for n, x in list(parts.items())})

    early = {0: sent[0]}
    spread(early, outer_bits)
    came = [swap(sent[step], step * span) for step in (1, 2)]

    sends, keeps = head_grad(
        turn, rates, mask, update_keys, update_values, others[0], fast_weights, 0, half, width
    )
    moved = [swap(sends[0], 2)]
    turn = after(turn, sends[0], *early.values())
    spread(early, [0])
    more_sends, more_keeps = head_grad(
        turn, rates, mask, update_keys, update_values, others[1], fast_weights, 1, half, width
    )
    turn = after(turn, more_sends[0], *came)
    keeps = [*keeps, *more_keeps]
    moved.append(swap(after(sends[1], more_sends[0]), 2))
    moved.append(swap(after(more_sends[0], turn), 2))
    came.append(swap(after(sent[3], turn), 3 * span))

    def cut(pair, b, side):
        rows = pair[0].shape[1] // 2
        return sum(
            lax.dynamic_slice_in_dim(x, side * rows, rows, 1).astype(f32) for x in pair
        )

    sums = []

    def settle(n):
        keep, got = keeps[n], after(moved[n], turn)
        for b in inner_bits[1:]:
            send = cut((keep, got), b, 1 - bit_of(b)).astype(bf16)
            keep, got = cut((keep, got), b, bit_of(b)), swap(send, 1 << b)
        total = keep + got.astype(f32)
        send = total.astype(bf16)
        sums.append((total, swap(send, span, lambda t: not matched(t))))
        return after(turn, send)

    turn = settle(0)
    turn = settle(1)
    moved.append(swap(after(more_sends[1], turn), 2))
    turn = after(turn, came[2], sums[0][1])
    turn = settle(2)
    turn = after(turn, sums[1][1])
    turn = settle(3)
    late = {0: jnp.stack([after(x, turn) for x in came])}
    spread(late, outer_bits)

    olds = [
        lax.dynamic_slice(
            fast_weights, (where[5], 0, where[6 + g] * share, 0), (1, 3, share, width)
        )[0]
        for g in range(2)
    ]
    upper = plane // 2 == 1
    held = []
    for g in range(2):
        low, high = (after(sums[n][0], turn) + sums[n][1].astype(f32) for n in (g, 2 + g))
        keep = jnp.where(upper, high, low)
        send = jnp.where(upper, low, high).astype(bf16)
        held.append((keep, swap(send, 2 * span, matched)))
        turn = after(turn, send)
    turn = after(turn, *early.values())
    fresh, far = [], []
    for g, (keep, got) in enumerate(held):
        new = renew(turn, keep, got, olds[g], step_sizes)
        turn = after(turn, new)
        for b in reversed(inner_bits[1:]):
            other = swap(new, 1 << b, matched)
            new = jnp.where(
                bit_of(b) == 1,
                jnp.concatenate([other, new], axis=1),
                jnp.concatenate([new, other], axis=1),
            )
        fresh.append(new)
        far.append(swap(new, 2, matched))
    late = {n: x if n == 0 else after(x, turn) for n, x in late.items()}
    spread(late, [0])

    pieces, slots = [], {}
    for e in sorted(early):
        slots[e] = (len(pieces), None)
        pieces.append(early[e])
        for step in range(1, heads):
            slots[step * span + e] = (len(pieces), step - 1)
        pieces.append(late[e])
    slots = [slots[n] for n in range(count)]
    rows = arrange(turn, pieces, slots, span, heads, width)
    attended = attend(turn, rows)
    far = [after(x, attended) for x in far]
    near = [swap(x, 1, matched) for x in fresh + far]
    blocks = finish(where, rows, attended, fresh + far + near, heads)
    got = [swap(x, step * span) if step else x for step, x in enumerate(blocks)]
    return join(where, got, heads, width)


def solution(mesh):
    rows = P(("groups", "tokens"), None)
    return jax.shard_map(
        on_device,
        mesh=mesh,
        in_specs=(
            rows,
            rows,
            rows,
            P(("groups", "tokens")),
            P(),
            P(),
            rows,
            rows,
            rows,
            P(("groups", "tokens")),
        ),
        out_specs=rows,
        check_vma=False,
    )
```

```python
import functools

import jax
import jax.numpy as jnp
from jax import lax
from jax.experimental import pallas as pl
from jax.experimental.pallas import tpu as pltpu
from jax.sharding import PartitionSpec as P

VIEW_ROWS = 128
AXIS = "tokens"
epsilon = 1e-05
f32 = jnp.float32
bf16 = jnp.bfloat16
i32 = jnp.int32
TAG_ROWS = 16
MIB = 1024 * 1024


def swap(value, mask, senders=None):
    count = lax.axis_size(AXIS)
    pairs = [(t, t ^ mask) for t in range(count) if senders is None or senders(t)]
    return lax.ppermute(value, AXIS, pairs)


def after(value, *others):
    return lax.optimization_barrier((value, *others))[0]


def head_of(plane, head_count):
    half = head_count // 2
    return (plane % 2) * half + plane // 2


def whole(shape):
    return pl.BlockSpec(shape, lambda i: (0,) * len(shape))


def position(span, heads):
    me = lax.axis_index(AXIS)
    plane, inner = me // span, me % span
    core = me % 2
    return (
        plane,
        core,
        (me // 2) % 2,
        me,
        inner,
        head_of(plane, heads),
        (plane % 2 == core).astype(i32),
    )


def call(body, name, inputs, specs, outs, out_specs=None, scratch=(), vmem=8, flops=0):
    return pl.pallas_call(
        body,
        name=name,
        grid=(1,),
        in_specs=specs,
        out_specs=out_specs or [whole(o.shape) for o in outs],
        scratch_shapes=list(scratch),
        out_shape=list(outs),
        cost_estimate=pl.CostEstimate(flops=flops, bytes_accessed=0, transcendentals=0),
        compiler_params=pltpu.CompilerParams(vmem_limit_bytes=vmem * MIB),
    )(*inputs)


def fetch_small(sources, buffers, sem):
    copies = [
        pltpu.make_async_copy(source, to, sem.at[n])
        for n, (source, to) in enumerate(zip(sources, buffers))
    ]
    for copy in copies:
        copy.start()
    return copies


def rate_column(rates, mask, head):
    at = lax.broadcasted_iota(i32, rates.shape, 0) == head
    row = jnp.sum(jnp.where(at, rates, 0.0), axis=0, keepdims=True) * mask.astype(f32)
    return -jnp.transpose(jnp.broadcast_to(row, (8, row.shape[1])))[:, 0:1]


def pack_body(span, heads, rates, mask, views, keys, values, *refs):
    half = heads // 2
    target, refs = refs[:3], refs[3:]
    packed, sent = refs[:half], refs[half : half + heads]
    rates_s, mask_s, views_s, value_s, pack_s, sent_s, in_sem, target_sem, out_sem = refs[
        half + heads :
    ]
    where = position(span, heads)
    rows, width = value_s.shape[1:]
    count = target[0].shape[0]

    def columns(head):
        return pl.ds(pl.multiple_of(head * width, width), width)

    small = fetch_small((rates, mask, views), (rates_s, mask_s, views_s), in_sem.at[half])
    loads = []
    for j in range(half):
        head = (1 - where[1]) * half + j
        for i, to in ((1, value_s.at[j]), (0, pack_s.at[j, 0])):
            source = (keys, values)[i]
            loads.append(pltpu.make_async_copy(source.at[:, columns(head)], to, in_sem.at[j, i]))
            loads[-1].start()
    rows_in = []
    for step in range(heads):
        head = head_of(where[0] ^ step, heads)
        for i in range(3):
            to = sent_s.at[step, pl.ds(i * count, count)]
            rows_in.append(
                pltpu.make_async_copy(
                    target[i].at[:, columns(head)], to, target_sem.at[step, i]
                )
            )
            rows_in[-1].start()
    for copy in small:
        copy.wait()
    row_at = lax.broadcasted_iota(i32, (TAG_ROWS, count), 0)
    ids = views_s[...]
    digits = jnp.where(row_at == 0, ids // 256, jnp.where(row_at == 1, ids % 256, 0))
    for step in range(heads):
        sent_s[step, pl.ds(3 * count, TAG_ROWS), :] = jnp.zeros((TAG_ROWS, width), bf16)
        sent_s[step, pl.ds(3 * count, TAG_ROWS), pl.ds(0, count)] = digits.astype(f32).astype(bf16)
    stores = []
    for j in range(half):
        rate = rate_column(rates_s[...], mask_s[...], (1 - where[1]) * half + j)
        loads[2 * j].wait()
        pack_s[j, 1] = (rate * value_s[j].astype(f32)).astype(bf16)
        loads[2 * j + 1].wait()
        stores.append(pltpu.make_async_copy(pack_s.at[j], packed[j], out_sem.at[j]))
        stores[-1].start()
    for step in range(heads):
        for i in range(3):
            rows_in[3 * step + i].wait()
        stores.append(pltpu.make_async_copy(sent_s.at[step], sent[step], out_sem.at[half + step]))
        stores[-1].start()
    for store in stores:
        store.wait()


def pack(rates, mask, views, keys, values, target, span, heads, width):
    half, rows, count = heads // 2, keys.shape[0], views.shape[1]
    small = (rates, mask, views)
    anywhere = pl.BlockSpec(memory_space=pl.ANY)
    piece = (3 * count + TAG_ROWS, width)
    outs = call(
        functools.partial(pack_body, span, heads),
        "pack",
        (*small, keys, values, *target),
        [anywhere] * 8,
        [jax.ShapeDtypeStruct((2, rows, width), bf16)] * half
        + [jax.ShapeDtypeStruct(piece, bf16)] * heads,
        out_specs=[anywhere] * (half + heads),
        scratch=[
            *[pltpu.VMEM(x.shape, x.dtype) for x in small],
            pltpu.VMEM((half, rows, width), bf16),
            pltpu.VMEM((half, 2, rows, width), bf16),
            pltpu.VMEM((heads, *piece), bf16),
            pltpu.SemaphoreType.DMA((half + 1, 3)),
            pltpu.SemaphoreType.DMA((heads, 3)),
            pltpu.SemaphoreType.DMA((half + heads,)),
        ],
        vmem=62,
    )
    return outs[:half], outs[half:]


def head_grad_body(span, heads, lane, rates, mask, keys, values, other, weights, *refs):
    rates_s, mask_s, k_s, v_s, w_s, tg_s, hidden_s, gate_s, up_s, full, send_s, keep_s = refs[-14:-2]
    in_sem, out_sem = refs[-2:]
    outs = refs[:-14]
    arrays = len(outs) // 2
    sends, keeps = outs[:arrays], outs[arrays:]
    rows, width = v_s.shape
    where = position(span, heads)
    head = where[1] * (heads // 2) + lane
    cols = pl.ds(pl.multiple_of(head * width, width), width)
    upper, lower = pl.ds(0, rows), pl.ds(rows, rows)
    loads = [
        pltpu.make_async_copy(keys.at[:, cols], k_s.at[upper], in_sem.at[0]),
        pltpu.make_async_copy(weights.at[head, 0], w_s.at[0], in_sem.at[1]),
        pltpu.make_async_copy(weights.at[head, 1], w_s.at[1], in_sem.at[2]),
        pltpu.make_async_copy(values.at[:, cols], v_s, in_sem.at[3]),
        pltpu.make_async_copy(weights.at[head, 2], w_s.at[2], in_sem.at[4]),
        pltpu.make_async_copy(other.at[0], k_s.at[lower], in_sem.at[5]),
        pltpu.make_async_copy(other.at[1], tg_s.at[lower], in_sem.at[6]),
    ]
    for load in loads:
        load.start()
    small = fetch_small((rates, mask), (rates_s, mask_s), in_sem.at[pl.ds(7, 2)])
    for copy in small:
        copy.wait()
    rate = rate_column(rates_s[...], mask_s[...], head)
    chunk = 256
    for at in range(0, 2 * rows, chunk):
        span = pl.ds(at, chunk)
        if at == 0:
            loads[0].wait()
            loads[1].wait()
        if at == rows:
            loads[5].wait()
        k = k_s[span, :]
        pre_gate = jnp.dot(k, w_s[0], preferred_element_type=f32)
        if at == 0:
            loads[2].wait()
        pre_up = jnp.dot(k, w_s[1], preferred_element_type=f32)
        if at == 0:
            loads[3].wait()
            loads[4].wait()
        if at == rows:
            loads[6].wait()
        if at < rows:
            tg = (rate[at : at + chunk] * v_s[span, :].astype(f32)).astype(bf16)
            tg_s[span, :] = tg
        else:
            tg = tg_s[span, :]
        back = lax.dot_general(tg, w_s[2], (((1,), (1,)), ((), ())), preferred_element_type=f32)
        sigma = 0.5 * jnp.tanh(0.5 * pre_gate) + 0.5
        activated = pre_gate * sigma
        hidden_s[span, :] = (activated * pre_up).astype(bf16)
        gate_s[span, :] = (back * pre_up * (sigma + activated * (1.0 - sigma))).astype(bf16)
        up_s[span, :] = (back * activated).astype(bf16)
    quarter = width // 4
    bit = where[2]
    stores = []
    for i, left, right in ((2, hidden_s, tg_s), (0, k_s, gate_s), (1, k_s, up_s)):
        full[...] = lax.dot_general(
            left[...], right[...], (((0,), (0,)), ((), ())), preferred_element_type=f32
        )
        for g in range(2):
            kept = pl.ds(pl.multiple_of(bit * 2 * quarter + g * quarter, quarter), quarter)
            sent = pl.ds(pl.multiple_of((1 - bit) * 2 * quarter + g * quarter, quarter), quarter)
            send_s[g, i] = full[sent, :].astype(bf16)
            keep_s[g, i] = full[kept, :]
            stores += [
                pltpu.make_async_copy(
                    send_s.at[g, i], sends[g % arrays].at[g // arrays, i], out_sem.at[0, g, i]
                ),
                pltpu.make_async_copy(
                    keep_s.at[g, i], keeps[g % arrays].at[g // arrays, i], out_sem.at[1, g, i]
                ),
            ]
            stores[-2].start()
            stores[-1].start()
    for store in stores:
        store.wait()


def head_grad(rates, mask, keys, values, other, weights, span, heads, lane, width, arrays):
    rows = keys.shape[0]
    shape = (3, width // 4, width)
    out = (2 // arrays, *shape)
    anywhere = pl.BlockSpec(memory_space=pl.ANY)
    in_hbm = pl.BlockSpec(memory_space=pltpu.HBM)
    both = pltpu.VMEM((2 * rows, width), bf16)
    outs = call(
        functools.partial(head_grad_body, span, heads, lane),
        "head_grad_%d" % lane,
        (rates, mask, keys, values, other, weights),
        [anywhere, anywhere, in_hbm, in_hbm, anywhere, in_hbm],
        [jax.ShapeDtypeStruct(out, bf16)] * arrays + [jax.ShapeDtypeStruct(out, f32)] * arrays,
        out_specs=[anywhere] * 2 * arrays,
        scratch=[
            pltpu.VMEM(rates.shape, f32),
            pltpu.VMEM(mask.shape, i32),
            both,
            pltpu.VMEM((rows, width), bf16),
            pltpu.VMEM((3, width, width), bf16),
            both,
            both,
            both,
            both,
            pltpu.VMEM((width, width), f32),
            pltpu.VMEM((2, *shape), bf16),
            pltpu.VMEM((2, *shape), f32),
            pltpu.SemaphoreType.DMA((9,)),
            pltpu.SemaphoreType.DMA((2, 2, 3)),
        ],
        vmem=62,
    )
    return outs[:arrays], outs[arrays:]


def arrange_body(slots, span, *refs):
    out = refs[-1]
    pieces = []
    for n, at in slots:
        pieces.append(refs[n] if at is None else refs[n].at[at])
    me = lax.axis_index(AXIS)
    inner = me % span
    rows = (pieces[0].shape[0] - TAG_ROWS) // 3
    count = len(pieces)
    heads = count // span
    tags = [p[pl.ds(3 * rows, TAG_ROWS), pl.ds(0, rows)].astype(f32) for p in pieces]
    ids = jnp.concatenate([t[0:1, :] * 256.0 + t[1:2, :] for t in tags], axis=0).astype(i32)
    square = (count, count)
    earlier = (
        (me ^ lax.broadcasted_iota(i32, square, 1)) < (me ^ lax.broadcasted_iota(i32, square, 0))
    ).astype(f32)
    before = (
        lax.broadcasted_iota(i32, (rows, rows), 0) < lax.broadcasted_iota(i32, (rows, rows), 1)
    ).astype(f32)
    place = jnp.full((count, rows), -1.0, f32)
    for j in range(heads):
        hit = (ids == j * span + inner).astype(f32)
        rank = jnp.dot(hit, before, preferred_element_type=f32) + jnp.sum(
            jnp.dot(earlier, hit, preferred_element_type=f32), axis=1, keepdims=True
        )
        place = jnp.where(hit > 0.0, rank + float(j * VIEW_ROWS), place)
    place = place.astype(i32)
    group = 4
    totals = [None] * 3
    for first in range(0, count, group):
        row_at = lax.broadcasted_iota(i32, (heads * VIEW_ROWS, rows), 0)
        pick = jnp.concatenate(
            [
                (row_at == place[n : n + 1, :]).astype(f32).astype(bf16)
                for n in range(first, first + group)
            ],
            axis=1,
        )
        for i in range(3):
            source = jnp.concatenate(
                [pieces[n][pl.ds(i * rows, rows), :] for n in range(first, first + group)],
                axis=0,
            )
            part = jnp.dot(pick, source, preferred_element_type=f32)
            totals[i] = part if totals[i] is None else totals[i] + part
    for i in range(3):
        out[i] = totals[i].astype(bf16)


def arrange(pieces, slots, span, heads, width):
    return call(
        functools.partial(arrange_body, slots, span),
        "arrange",
        tuple(pieces),
        [whole(x.shape) for x in pieces],
        [jax.ShapeDtypeStruct((3, heads * VIEW_ROWS, width), bf16)],
        vmem=20,
    )[0]


def attend_body(rows, attended):
    width = rows.shape[2]
    for v in range(rows.shape[1] // VIEW_ROWS):
        at = pl.ds(v * VIEW_ROWS, VIEW_ROWS)
        scores = lax.dot_general(
            rows[0, at, :], rows[1, at, :], (((1,), (1,)), ((), ())), preferred_element_type=f32
        ) * width ** (-0.5)
        top = jnp.max(scores, axis=1, keepdims=True)
        raised = jnp.exp(scores - top)
        probs = (raised / jnp.sum(raised, axis=1, keepdims=True)).astype(bf16)
        attended[at, :] = jnp.dot(probs, rows[2, at, :], preferred_element_type=f32)


def attend(rows):
    return call(
        attend_body,
        "attend",
        (rows,),
        [whole(rows.shape)],
        [jax.ShapeDtypeStruct(rows.shape[1:], f32)],
    )[0]


def add_body(keep, got, total, send):
    total[...] = keep[...] + got[...].astype(f32)
    send[...] = total[...].astype(bf16)


def add(keep, got):
    return call(
        add_body,
        "add",
        (keep, got),
        [whole(keep.shape)] * 2,
        [jax.ShapeDtypeStruct(keep.shape, t) for t in (f32, bf16)],
        flops=9000000000,
    )


def hand_over_body(span, *refs):
    upper = lax.axis_index(AXIS) // span // 2 == 1
    sources, sends, keeps, total_s, got_s, sem = refs[:4], refs[4], refs[5], *refs[6:]

    def fetch(first, second):
        copies = []
        for n, pair in enumerate((first, second)):
            for i, (source, to) in enumerate(zip(pair, (total_s, got_s))):
                copies.append(pltpu.make_async_copy(source, to.at[n], sem.at[n, i]))
                copies[-1].start()
        for copy in copies:
            copy.wait()

    @pl.when(upper)
    def _():
        fetch(sources[:2], sources[2:])

    @pl.when(jnp.logical_not(upper))
    def _():
        fetch(sources[2:], sources[:2])

    sends[...] = (total_s[0] + got_s[0].astype(f32)).astype(bf16)
    keeps[...] = total_s[1] + got_s[1].astype(f32)


def hand_over(low, high, span):
    shape = low[0].shape
    sources = (*low, *high)
    return call(
        functools.partial(hand_over_body, span),
        "hand_over",
        sources,
        [pl.BlockSpec(memory_space=pl.ANY)] * 4,
        [jax.ShapeDtypeStruct(shape, bf16), jax.ShapeDtypeStruct(shape, f32)],
        scratch=[
            pltpu.VMEM((2, *shape), f32),
            pltpu.VMEM((2, *shape), bf16),
            pltpu.SemaphoreType.DMA((2, 2)),
        ],
    )


def renew_body(span, heads, keep, got, old, steps, *refs):
    *earlier, fresh = refs
    step = jnp.where(
        lax.broadcasted_iota(i32, steps.shape, 1) == position(span, heads)[5], steps[...], 0.0
    )
    step = jnp.sum(step, axis=1, keepdims=True)
    total = keep[...] + got[...].astype(f32)
    scale = lax.rsqrt(jnp.mean(total * total, axis=-1, keepdims=True) + epsilon)
    new = (old[...].astype(f32) - step * (total * scale)).astype(bf16)
    if earlier:
        fresh[pl.ds(0, 1)] = earlier[0][...]
        fresh[pl.ds(1, 1)] = new
    else:
        fresh[...] = new


def renew(keep, got, old, steps, span, heads, *earlier):
    shape = (keep.shape[0] + len(earlier), *keep.shape[1:])
    inputs = (keep, got, old, steps, *earlier)
    return call(
        functools.partial(renew_body, span, heads),
        "renew_%d" % len(earlier),
        inputs,
        [whole(x.shape) for x in inputs],
        [jax.ShapeDtypeStruct(shape, bf16)],
    )[0]


def finish_body(span, heads, steps, rows, attended, *refs):
    weights = refs[:4]
    outs, full = refs[4:-1], refs[-1]
    where = position(span, heads)
    bit, is_owner = where[2], where[6]
    quarter = weights[0].shape[2]

    def place(blocks):
        for side, block in enumerate(blocks):
            half = bit if side == 0 else 1 - bit
            for g in range(2):
                at = pl.ds(pl.multiple_of(half * 2 * quarter + g * quarter, quarter), quarter)
                for i in range(3):
                    full[i, at, :] = block[g, i]

    @pl.when(is_owner == 1)
    def _():
        place(weights[:2])

    @pl.when(is_owner == 0)
    def _():
        place(weights[2:])

    for step, out in zip(steps, outs):
        at = pl.ds(pl.multiple_of((where[0] ^ step) * VIEW_ROWS, VIEW_ROWS), VIEW_ROWS)
        q = rows[0, at, :]
        pre_gate = jnp.dot(q, full[0], preferred_element_type=f32)
        pre_up = jnp.dot(q, full[1], preferred_element_type=f32)
        hidden = (pre_gate * jax.nn.sigmoid(pre_gate) * pre_up).astype(bf16)
        fast = jnp.dot(hidden, full[2], preferred_element_type=f32)
        scale = lax.rsqrt(jnp.mean(fast * fast, axis=-1, keepdims=True) + epsilon)
        out[...] = (fast * scale + attended[at, :]).astype(bf16)


def finish(rows, attended, weights, span, heads, steps):
    width = rows.shape[2]
    inputs = (rows, attended, *weights)
    return call(
        functools.partial(finish_body, span, heads, steps),
        "finish_%d" % steps[0],
        inputs,
        [pl.BlockSpec((1, *rows.shape[1:]), lambda i: (0, 0, 0))]
        + [whole(x.shape) for x in inputs[1:]],
        [jax.ShapeDtypeStruct((VIEW_ROWS, width), bf16)] * len(steps),
        scratch=[pltpu.VMEM((3, width, width), bf16)],
        vmem=12,
    )


def join_body(span, heads, width, *refs):
    out = refs[-1]
    plane = lax.axis_index(AXIS) // span
    for step in range(heads):
        head = head_of(plane ^ step, heads)
        out[:, pl.ds(pl.multiple_of(head * width, width), width)] = refs[step][...]


def join(blocks, span, heads, width):
    rows = blocks[0].shape[0]
    return call(
        functools.partial(join_body, span, heads, width),
        "join",
        tuple(blocks),
        [whole(x.shape) for x in blocks],
        [jax.ShapeDtypeStruct((rows, heads * width), bf16)],
    )[0]


def on_device(
    update_keys,
    update_values,
    update_rates,
    update_mask,
    fast_weights,
    step_sizes,
    target_queries,
    target_keys,
    target_values,
    target_views,
):
    heads, _, width, _ = fast_weights.shape
    half = heads // 2
    count = lax.axis_size(AXIS)
    me = lax.axis_index(AXIS)
    span = count // heads
    plane, inner = me // span, me % span
    core = inner % 2
    inner_bits = list(range(1, span.bit_length() - 1))
    bit_of = lambda b: (me >> b) & 1
    matched = lambda t: (t // span) % 2 == t % 2

    share = width // 4 // 2 ** (len(inner_bits) - 1)
    first = [bit_of(1) * 2 + g for g in range(2)]
    for b in inner_bits[1:]:
        first = [2 * f + bit_of(b) for f in first]

    rates, mask = update_rates.T, update_mask[None, :]
    steps = step_sizes[None, :]

    others, sent = pack(
        rates,
        mask,
        target_views[None, :],
        update_keys,
        update_values,
        (target_queries, target_keys, target_values),
        span,
        heads,
        width,
    )
    turn = [sent[0]]
    others = [swap(x, 1) for x in others]

    outer_bits = list(reversed(inner_bits))

    def spread(parts, bits):
        for b in bits:
            parts.update({n | (1 << b): swap(x, 1 << b) for n, x in list(parts.items())})

    early = {0: sent[0]}
    spread(early, outer_bits)
    came = [swap(sent[step], step * span) for step in (1, 2)]

    grad_inputs = (mask, update_keys, update_values)
    sends, keeps = head_grad(
        after(rates, *turn), *grad_inputs, others[0], fast_weights, span, heads, 0, width, 2
    )
    turn = [sends[0], *early.values()]
    spread(early, [0])
    more_sends, more_keeps = head_grad(
        after(rates, *turn), *grad_inputs, others[1], fast_weights, span, heads, 1, width, 2
    )
    turn = [more_sends[0], *came]
    keeps = [*keeps, *more_keeps]
    moved = [
        swap(sends[0], 2),
        swap(after(sends[1], more_sends[0]), 2),
        swap(after(more_sends[0], *turn[1:]), 2),
    ]
    came.append(swap(after(sent[3], *turn), 3 * span))

    def cut(pair, b, side):
        rows = pair[0].shape[2] // 2
        return sum(
            lax.dynamic_slice_in_dim(x, side * rows, rows, 2).astype(f32) for x in pair
        )

    sums = []

    def settle(n):
        keep, got = keeps[n], after(moved[n], *turn)
        for b in inner_bits[1:]:
            send = cut((keep, got), b, 1 - bit_of(b)).astype(bf16)
            keep, got = cut((keep, got), b, bit_of(b)), swap(send, 1 << b)
        total, send = add(keep, got)
        sums.append((total, send))
        if n >= 2:
            both = swap(
                jnp.concatenate([sums[n - 2][1], send]), span, lambda t: not matched(t)
            )
            sums[n - 2], sums[n] = (sums[n - 2][0], both[:1]), (total, both[1:])
        return [send]

    turn = settle(0)
    turn = settle(1)
    moved.append(swap(after(more_sends[1], *turn), 2))
    turn += [came[2]]
    turn = settle(2)
    turn = settle(3)
    late = {0: jnp.stack([after(x, *turn) for x in came])}
    spread(late, outer_bits)

    olds = [
        lax.dynamic_slice(
            fast_weights, (head_of(plane, heads), 0, first[g] * share, 0), (1, 3, share, width)
        )
        for g in range(2)
    ]
    held = []
    for g in range(2):
        low = (after(sums[g][0], *turn), sums[g][1])
        send, keep = hand_over(low, sums[2 + g], span)
        held.append((keep, swap(send, 2 * span, matched)))
        turn = [send]
    turn += early.values()
    fresh = renew(after(held[0][0], *turn), held[0][1], olds[0], steps, span, heads)
    fresh = renew(*held[1], olds[1], steps, span, heads, fresh)
    turn = [fresh]
    for b in reversed(inner_bits[1:]):
        other = swap(fresh, 1 << b, matched)
        fresh = jnp.where(
            bit_of(b) == 1,
            jnp.concatenate([other, fresh], axis=2),
            jnp.concatenate([fresh, other], axis=2),
        )
    far = swap(fresh, 2, matched)
    late = {n: x if n == 0 else after(x, *turn) for n, x in late.items()}
    spread(late, [0])

    pieces, slots = [], {}
    for e in sorted(early):
        slots[e] = (len(pieces), None)
        pieces.append(early[e])
        for step in range(1, heads):
            slots[step * span + e] = (len(pieces), step - 1)
        pieces.append(late[e])
    slots = [slots[n] for n in range(count)]
    rows = arrange([after(pieces[0], *turn), *pieces[1:]], slots, span, heads, width)
    attended = attend(rows)
    far = after(far, attended)
    weights = [fresh, far, swap(fresh, 1, matched), swap(far, 1, matched)]
    split = heads // 2
    far_blocks = finish(rows, attended, weights, span, heads, tuple(range(split, heads)))
    got = [swap(x, (split + n) * span) for n, x in enumerate(far_blocks)]
    near_blocks = finish(
        after(rows, far_blocks[0]), attended, weights, span, heads, tuple(range(split))
    )
    got = [swap(x, step * span) if step else x for step, x in enumerate(near_blocks)] + got
    return join(got, span, heads, width)


def solution(mesh):
    rows = P(("groups", "tokens"), None)
    return jax.shard_map(
        on_device,
        mesh=mesh,
        in_specs=(
            rows,
            rows,
            rows,
            P(("groups", "tokens")),
            P(),
            P(),
            rows,
            rows,
            rows,
            P(("groups", "tokens")),
        ),
        out_specs=rows,
        check_vma=False,
    )
```

```python
import functools

import jax
import jax.numpy as jnp
from jax import lax
from jax.experimental import pallas as pl
from jax.experimental.pallas import tpu as pltpu
from jax.sharding import PartitionSpec as P

VIEW_ROWS = 128
AXIS = "tokens"
epsilon = 1e-05
f32 = jnp.float32
bf16 = jnp.bfloat16
i32 = jnp.int32
TAG_ROWS = 16
MIB = 1024 * 1024


def swap(value, mask, senders=None):
    count = lax.axis_size(AXIS)
    pairs = [(t, t ^ mask) for t in range(count) if senders is None or senders(t)]
    return lax.ppermute(value, AXIS, pairs)


def after(value, *others):
    return lax.optimization_barrier((value, *others))[0]


def head_of(plane, head_count):
    half = head_count // 2
    return (plane % 2) * half + plane // 2


def whole(shape):
    return pl.BlockSpec(shape, lambda i: (0,) * len(shape))


def position(span, heads):
    me = lax.axis_index(AXIS)
    plane, inner = me // span, me % span
    core = me % 2
    return (
        plane,
        core,
        (me // 2) % 2,
        me,
        inner,
        head_of(plane, heads),
        (plane % 2 == core).astype(i32),
    )


def call(body, name, inputs, specs, outs, out_specs=None, scratch=(), vmem=8, flops=0):
    return pl.pallas_call(
        body,
        name=name,
        grid=(1,),
        in_specs=specs,
        out_specs=out_specs or [whole(o.shape) for o in outs],
        scratch_shapes=list(scratch),
        out_shape=list(outs),
        cost_estimate=pl.CostEstimate(flops=flops, bytes_accessed=0, transcendentals=0),
        compiler_params=pltpu.CompilerParams(vmem_limit_bytes=vmem * MIB),
    )(*inputs)


def fetch_small(sources, buffers, sem):
    copies = [
        pltpu.make_async_copy(source, to, sem.at[n])
        for n, (source, to) in enumerate(zip(sources, buffers))
    ]
    for copy in copies:
        copy.start()
    return copies


def rate_column(rates, mask, head):
    at = lax.broadcasted_iota(i32, rates.shape, 0) == head
    row = jnp.sum(jnp.where(at, rates, 0.0), axis=0, keepdims=True) * mask.astype(f32)
    return -jnp.transpose(jnp.broadcast_to(row, (8, row.shape[1])))[:, 0:1]


def pack_body(span, heads, rates, mask, views, keys, values, *refs):
    half = heads // 2
    target, refs = refs[:3], refs[3:]
    packed, sent = refs[:half], refs[half : half + heads]
    rates_s, mask_s, views_s, value_s, pack_s, sent_s, in_sem, target_sem, out_sem = refs[
        half + heads :
    ]
    where = position(span, heads)
    rows, width = value_s.shape[1:]
    count = target[0].shape[0]

    def columns(head):
        return pl.ds(pl.multiple_of(head * width, width), width)

    small = fetch_small((rates, mask, views), (rates_s, mask_s, views_s), in_sem.at[half])
    loads = []
    for j in range(half):
        head = (1 - where[1]) * half + j
        for i, to in ((1, value_s.at[j]), (0, pack_s.at[j, 0])):
            source = (keys, values)[i]
            loads.append(pltpu.make_async_copy(source.at[:, columns(head)], to, in_sem.at[j, i]))
            loads[-1].start()
    rows_in = []
    for step in range(heads):
        head = head_of(where[0] ^ step, heads)
        for i in range(3):
            to = sent_s.at[step, pl.ds(i * count, count)]
            rows_in.append(
                pltpu.make_async_copy(
                    target[i].at[:, columns(head)], to, target_sem.at[step, i]
                )
            )
            rows_in[-1].start()
    for copy in small:
        copy.wait()
    row_at = lax.broadcasted_iota(i32, (TAG_ROWS, count), 0)
    ids = views_s[...]
    digits = jnp.where(row_at == 0, ids // 256, jnp.where(row_at == 1, ids % 256, 0))
    for step in range(heads):
        sent_s[step, pl.ds(3 * count, TAG_ROWS), :] = jnp.zeros((TAG_ROWS, width), bf16)
        sent_s[step, pl.ds(3 * count, TAG_ROWS), pl.ds(0, count)] = digits.astype(f32).astype(bf16)
    stores = []
    for j in range(half):
        rate = rate_column(rates_s[...], mask_s[...], (1 - where[1]) * half + j)
        loads[2 * j].wait()
        pack_s[j, 1] = (rate * value_s[j].astype(f32)).astype(bf16)
        loads[2 * j + 1].wait()
        stores.append(pltpu.make_async_copy(pack_s.at[j], packed[j], out_sem.at[j]))
        stores[-1].start()
    for step in range(heads):
        for i in range(3):
            rows_in[3 * step + i].wait()
        stores.append(pltpu.make_async_copy(sent_s.at[step], sent[step], out_sem.at[half + step]))
        stores[-1].start()
    for store in stores:
        store.wait()


def pack(rates, mask, views, keys, values, target, span, heads, width):
    half, rows, count = heads // 2, keys.shape[0], views.shape[1]
    small = (rates, mask, views)
    anywhere = pl.BlockSpec(memory_space=pl.ANY)
    piece = (3 * count + TAG_ROWS, width)
    outs = call(
        functools.partial(pack_body, span, heads),
        "pack",
        (*small, keys, values, *target),
        [anywhere] * 8,
        [jax.ShapeDtypeStruct((2, rows, width), bf16)] * half
        + [jax.ShapeDtypeStruct(piece, bf16)] * heads,
        out_specs=[anywhere] * (half + heads),
        scratch=[
            *[pltpu.VMEM(x.shape, x.dtype) for x in small],
            pltpu.VMEM((half, rows, width), bf16),
            pltpu.VMEM((half, 2, rows, width), bf16),
            pltpu.VMEM((heads, *piece), bf16),
            pltpu.SemaphoreType.DMA((half + 1, 3)),
            pltpu.SemaphoreType.DMA((heads, 3)),
            pltpu.SemaphoreType.DMA((half + heads,)),
        ],
        vmem=62,
    )
    return outs[:half], outs[half:]


def head_grad_body(span, heads, lane, rates, mask, keys, values, other, weights, *refs):
    rates_s, mask_s, k_s, v_s, w_s, tg_s, hidden_s, gate_s, up_s, full, send_s, keep_s = refs[-14:-2]
    in_sem, out_sem = refs[-2:]
    outs = refs[:-14]
    arrays = len(outs) // 2
    sends, keeps = outs[:arrays], outs[arrays:]
    rows, width = v_s.shape
    where = position(span, heads)
    head = where[1] * (heads // 2) + lane
    cols = pl.ds(pl.multiple_of(head * width, width), width)
    upper, lower = pl.ds(0, rows), pl.ds(rows, rows)
    loads = [
        pltpu.make_async_copy(keys.at[:, cols], k_s.at[upper], in_sem.at[0]),
        pltpu.make_async_copy(weights.at[head, 0], w_s.at[0], in_sem.at[1]),
        pltpu.make_async_copy(weights.at[head, 1], w_s.at[1], in_sem.at[2]),
        pltpu.make_async_copy(values.at[:, cols], v_s, in_sem.at[3]),
        pltpu.make_async_copy(weights.at[head, 2], w_s.at[2], in_sem.at[4]),
        pltpu.make_async_copy(other.at[0], k_s.at[lower], in_sem.at[5]),
        pltpu.make_async_copy(other.at[1], tg_s.at[lower], in_sem.at[6]),
    ]
    small = fetch_small((rates, mask), (rates_s, mask_s), in_sem.at[pl.ds(7, 2)])
    for load in loads[:2]:
        load.start()
    for copy in small:
        copy.wait()
    for load in loads[2:]:
        load.start()
    rate = rate_column(rates_s[...], mask_s[...], head)
    chunk = 256
    for at in range(0, 2 * rows, chunk):
        span = pl.ds(at, chunk)
        if at == 0:
            loads[0].wait()
            loads[1].wait()
        if at == rows:
            loads[5].wait()
        k = k_s[span, :]
        pre_gate = jnp.dot(k, w_s[0], preferred_element_type=f32)
        if at == 0:
            loads[2].wait()
        pre_up = jnp.dot(k, w_s[1], preferred_element_type=f32)
        if at == 0:
            loads[3].wait()
            loads[4].wait()
        if at == rows:
            loads[6].wait()
        if at < rows:
            tg = (rate[at : at + chunk] * v_s[span, :].astype(f32)).astype(bf16)
            tg_s[span, :] = tg
        else:
            tg = tg_s[span, :]
        back = lax.dot_general(tg, w_s[2], (((1,), (1,)), ((), ())), preferred_element_type=f32)
        sigma = 0.5 * jnp.tanh(0.5 * pre_gate) + 0.5
        activated = pre_gate * sigma
        hidden_s[span, :] = (activated * pre_up).astype(bf16)
        gate_s[span, :] = (back * pre_up * (sigma + activated * (1.0 - sigma))).astype(bf16)
        up_s[span, :] = (back * activated).astype(bf16)
    quarter = width // 4
    bit = where[2]
    stores = []
    for i, left, right in ((2, hidden_s, tg_s), (0, k_s, gate_s), (1, k_s, up_s)):
        full[...] = lax.dot_general(
            left[...], right[...], (((0,), (0,)), ((), ())), preferred_element_type=f32
        )
        for g in range(2):
            kept = pl.ds(pl.multiple_of(bit * 2 * quarter + g * quarter, quarter), quarter)
            sent = pl.ds(pl.multiple_of((1 - bit) * 2 * quarter + g * quarter, quarter), quarter)
            send_s[g, i] = full[sent, :].astype(bf16)
            keep_s[g, i] = full[kept, :]
            stores += [
                pltpu.make_async_copy(
                    send_s.at[g, i], sends[g % arrays].at[g // arrays, i], out_sem.at[0, g, i]
                ),
                pltpu.make_async_copy(
                    keep_s.at[g, i], keeps[g % arrays].at[g // arrays, i], out_sem.at[1, g, i]
                ),
            ]
            stores[-2].start()
            stores[-1].start()
    for store in stores:
        store.wait()


def head_grad(rates, mask, keys, values, other, weights, span, heads, lane, width, arrays):
    rows = keys.shape[0]
    shape = (3, width // 4, width)
    out = (2 // arrays, *shape)
    anywhere = pl.BlockSpec(memory_space=pl.ANY)
    in_hbm = pl.BlockSpec(memory_space=pltpu.HBM)
    both = pltpu.VMEM((2 * rows, width), bf16)
    outs = call(
        functools.partial(head_grad_body, span, heads, lane),
        "head_grad_%d" % lane,
        (rates, mask, keys, values, other, weights),
        [anywhere, anywhere, in_hbm, in_hbm, anywhere, in_hbm],
        [jax.ShapeDtypeStruct(out, bf16)] * arrays + [jax.ShapeDtypeStruct(out, f32)] * arrays,
        out_specs=[anywhere] * 2 * arrays,
        scratch=[
            pltpu.VMEM(rates.shape, f32),
            pltpu.VMEM(mask.shape, i32),
            both,
            pltpu.VMEM((rows, width), bf16),
            pltpu.VMEM((3, width, width), bf16),
            both,
            both,
            both,
            both,
            pltpu.VMEM((width, width), f32),
            pltpu.VMEM((2, *shape), bf16),
            pltpu.VMEM((2, *shape), f32),
            pltpu.SemaphoreType.DMA((9,)),
            pltpu.SemaphoreType.DMA((2, 2, 3)),
        ],
        vmem=62,
    )
    return outs[:arrays], outs[arrays:]


def arrange_body(slots, span, *refs):
    out = refs[-1]
    pieces = []
    for n, at in slots:
        pieces.append(refs[n] if at is None else refs[n].at[at])
    me = lax.axis_index(AXIS)
    inner = me % span
    rows = (pieces[0].shape[0] - TAG_ROWS) // 3
    count = len(pieces)
    heads = count // span
    tags = [p[pl.ds(3 * rows, TAG_ROWS), pl.ds(0, rows)].astype(f32) for p in pieces]
    ids = jnp.concatenate([t[0:1, :] * 256.0 + t[1:2, :] for t in tags], axis=0).astype(i32)
    square = (count, count)
    earlier = (
        (me ^ lax.broadcasted_iota(i32, square, 1)) < (me ^ lax.broadcasted_iota(i32, square, 0))
    ).astype(f32)
    before = (
        lax.broadcasted_iota(i32, (rows, rows), 0) < lax.broadcasted_iota(i32, (rows, rows), 1)
    ).astype(f32)
    place = jnp.full((count, rows), -1.0, f32)
    for j in range(heads):
        hit = (ids == j * span + inner).astype(f32)
        rank = jnp.dot(hit, before, preferred_element_type=f32) + jnp.sum(
            jnp.dot(earlier, hit, preferred_element_type=f32), axis=1, keepdims=True
        )
        place = jnp.where(hit > 0.0, rank + float(j * VIEW_ROWS), place)
    place = place.astype(i32)
    group = 4
    totals = [None] * 3
    for first in range(0, count, group):
        row_at = lax.broadcasted_iota(i32, (heads * VIEW_ROWS, rows), 0)
        pick = jnp.concatenate(
            [
                (row_at == place[n : n + 1, :]).astype(f32).astype(bf16)
                for n in range(first, first + group)
            ],
            axis=1,
        )
        for i in range(3):
            source = jnp.concatenate(
                [pieces[n][pl.ds(i * rows, rows), :] for n in range(first, first + group)],
                axis=0,
            )
            part = jnp.dot(pick, source, preferred_element_type=f32)
            totals[i] = part if totals[i] is None else totals[i] + part
    for i in range(3):
        out[i] = totals[i].astype(bf16)


def arrange(pieces, slots, span, heads, width):
    return call(
        functools.partial(arrange_body, slots, span),
        "arrange",
        tuple(pieces),
        [whole(x.shape) for x in pieces],
        [jax.ShapeDtypeStruct((3, heads * VIEW_ROWS, width), bf16)],
        vmem=20,
    )[0]


def attend_body(rows, attended):
    width = rows.shape[2]
    for v in range(rows.shape[1] // VIEW_ROWS):
        at = pl.ds(v * VIEW_ROWS, VIEW_ROWS)
        scores = lax.dot_general(
            rows[0, at, :], rows[1, at, :], (((1,), (1,)), ((), ())), preferred_element_type=f32
        ) * width ** (-0.5)
        top = jnp.max(scores, axis=1, keepdims=True)
        raised = jnp.exp(scores - top)
        probs = (raised / jnp.sum(raised, axis=1, keepdims=True)).astype(bf16)
        attended[at, :] = jnp.dot(probs, rows[2, at, :], preferred_element_type=f32)


def attend(rows):
    return call(
        attend_body,
        "attend",
        (rows,),
        [whole(rows.shape)],
        [jax.ShapeDtypeStruct(rows.shape[1:], f32)],
    )[0]


def add_body(keep, got, total, send):
    total[...] = keep[...] + got[...].astype(f32)
    send[...] = total[...].astype(bf16)


def add(keep, got):
    return call(
        add_body,
        "add",
        (keep, got),
        [whole(keep.shape)] * 2,
        [jax.ShapeDtypeStruct(keep.shape, t) for t in (f32, bf16)],
        flops=2000000000,
    )


def hand_over_body(span, *refs):
    upper = lax.axis_index(AXIS) // span // 2 == 1
    sources, sends, keeps, total_s, got_s, sem = refs[:4], refs[4], refs[5], *refs[6:]

    def fetch(first, second):
        copies = []
        for n, pair in enumerate((first, second)):
            for i, (source, to) in enumerate(zip(pair, (total_s, got_s))):
                copies.append(pltpu.make_async_copy(source, to.at[n], sem.at[n, i]))
                copies[-1].start()
        for copy in copies:
            copy.wait()

    @pl.when(upper)
    def _():
        fetch(sources[:2], sources[2:])

    @pl.when(jnp.logical_not(upper))
    def _():
        fetch(sources[2:], sources[:2])

    sends[...] = (total_s[0] + got_s[0].astype(f32)).astype(bf16)
    keeps[...] = total_s[1] + got_s[1].astype(f32)


def hand_over(low, high, span):
    shape = low[0].shape
    sources = (*low, *high)
    return call(
        functools.partial(hand_over_body, span),
        "hand_over",
        sources,
        [pl.BlockSpec(memory_space=pl.ANY)] * 4,
        [jax.ShapeDtypeStruct(shape, bf16), jax.ShapeDtypeStruct(shape, f32)],
        scratch=[
            pltpu.VMEM((2, *shape), f32),
            pltpu.VMEM((2, *shape), bf16),
            pltpu.SemaphoreType.DMA((2, 2)),
        ],
        flops=4000000000,
    )


def renew_body(span, heads, keep, got, old, steps, *refs):
    *earlier, fresh = refs
    step = jnp.where(
        lax.broadcasted_iota(i32, steps.shape, 1) == position(span, heads)[5], steps[...], 0.0
    )
    step = jnp.sum(step, axis=1, keepdims=True)
    total = keep[...] + got[...].astype(f32)
    scale = lax.rsqrt(jnp.mean(total * total, axis=-1, keepdims=True) + epsilon)
    new = (old[...].astype(f32) - step * (total * scale)).astype(bf16)
    if earlier:
        fresh[pl.ds(0, 1)] = earlier[0][...]
        fresh[pl.ds(1, 1)] = new
    else:
        fresh[...] = new


def renew(keep, got, old, steps, span, heads, *earlier):
    shape = (keep.shape[0] + len(earlier), *keep.shape[1:])
    inputs = (keep, got, old, steps, *earlier)
    return call(
        functools.partial(renew_body, span, heads),
        "renew_%d" % len(earlier),
        inputs,
        [whole(x.shape) for x in inputs],
        [jax.ShapeDtypeStruct(shape, bf16)],
    )[0]


def finish_body(span, heads, steps, rows, attended, *refs):
    weights = refs[:4]
    outs, full = refs[4:-1], refs[-1]
    where = position(span, heads)
    bit, is_owner = where[2], where[6]
    quarter = weights[0].shape[2]

    def place(blocks):
        for side, block in enumerate(blocks):
            half = bit if side == 0 else 1 - bit
            for g in range(2):
                at = pl.ds(pl.multiple_of(half * 2 * quarter + g * quarter, quarter), quarter)
                for i in range(3):
                    full[i, at, :] = block[g, i]

    @pl.when(is_owner == 1)
    def _():
        place(weights[:2])

    @pl.when(is_owner == 0)
    def _():
        place(weights[2:])

    for step, out in zip(steps, outs):
        at = pl.ds(pl.multiple_of((where[0] ^ step) * VIEW_ROWS, VIEW_ROWS), VIEW_ROWS)
        q = rows[0, at, :]
        pre_gate = jnp.dot(q, full[0], preferred_element_type=f32)
        pre_up = jnp.dot(q, full[1], preferred_element_type=f32)
        hidden = (pre_gate * jax.nn.sigmoid(pre_gate) * pre_up).astype(bf16)
        fast = jnp.dot(hidden, full[2], preferred_element_type=f32)
        scale = lax.rsqrt(jnp.mean(fast * fast, axis=-1, keepdims=True) + epsilon)
        out[...] = (fast * scale + attended[at, :]).astype(bf16)


def finish(rows, attended, weights, span, heads, steps):
    width = rows.shape[2]
    inputs = (rows, attended, *weights)
    return call(
        functools.partial(finish_body, span, heads, steps),
        "finish_%d" % steps[0],
        inputs,
        [pl.BlockSpec((1, *rows.shape[1:]), lambda i: (0, 0, 0))]
        + [whole(x.shape) for x in inputs[1:]],
        [jax.ShapeDtypeStruct((VIEW_ROWS, width), bf16)] * len(steps),
        scratch=[pltpu.VMEM((3, width, width), bf16)],
        vmem=12,
    )


def join_body(span, heads, width, *refs):
    out = refs[-1]
    plane = lax.axis_index(AXIS) // span
    for step in range(heads):
        head = head_of(plane ^ step, heads)
        out[:, pl.ds(pl.multiple_of(head * width, width), width)] = refs[step][...]


def join(blocks, span, heads, width):
    rows = blocks[0].shape[0]
    return call(
        functools.partial(join_body, span, heads, width),
        "join",
        tuple(blocks),
        [whole(x.shape) for x in blocks],
        [jax.ShapeDtypeStruct((rows, heads * width), bf16)],
    )[0]


def on_device(
    update_keys,
    update_values,
    update_rates,
    update_mask,
    fast_weights,
    step_sizes,
    target_queries,
    target_keys,
    target_values,
    target_views,
):
    heads, _, width, _ = fast_weights.shape
    half = heads // 2
    count = lax.axis_size(AXIS)
    me = lax.axis_index(AXIS)
    span = count // heads
    plane, inner = me // span, me % span
    core = inner % 2
    inner_bits = list(range(1, span.bit_length() - 1))
    bit_of = lambda b: (me >> b) & 1
    matched = lambda t: (t // span) % 2 == t % 2

    share = width // 4 // 2 ** (len(inner_bits) - 1)
    first = [bit_of(1) * 2 + g for g in range(2)]
    for b in inner_bits[1:]:
        first = [2 * f + bit_of(b) for f in first]

    rates, mask = update_rates.T, update_mask[None, :]
    steps = step_sizes[None, :]

    others, sent = pack(
        rates,
        mask,
        target_views[None, :],
        update_keys,
        update_values,
        (target_queries, target_keys, target_values),
        span,
        heads,
        width,
    )
    turn = [sent[0]]
    others = [swap(x, 1) for x in others]

    outer_bits = list(reversed(inner_bits))

    def spread(parts, bits):
        for b in bits:
            parts.update({n | (1 << b): swap(x, 1 << b) for n, x in list(parts.items())})

    early = {0: sent[0]}
    spread(early, outer_bits)
    came = [swap(sent[step], step * span) for step in (1, 2)]

    grad_inputs = (mask, update_keys, update_values)
    sends, keeps = head_grad(
        after(rates, *turn), *grad_inputs, others[0], fast_weights, span, heads, 0, width, 2
    )
    turn = [sends[0], *early.values()]
    spread(early, [0])
    more_sends, more_keeps = head_grad(
        after(rates, *turn), *grad_inputs, others[1], fast_weights, span, heads, 1, width, 2
    )
    turn = [more_sends[0], *came]
    keeps = [*keeps, *more_keeps]
    moved = [
        swap(sends[0], 2),
        swap(after(sends[1], more_sends[0]), 2),
        swap(after(more_sends[0], *turn[1:]), 2),
    ]
    came.append(swap(after(sent[3], *turn), 3 * span))

    def cut(pair, b, side):
        rows = pair[0].shape[2] // 2
        return sum(
            lax.dynamic_slice_in_dim(x, side * rows, rows, 2).astype(f32) for x in pair
        )

    sums = []

    def settle(n):
        keep, got = keeps[n], after(moved[n], *turn)
        for b in inner_bits[1:]:
            send = cut((keep, got), b, 1 - bit_of(b)).astype(bf16)
            keep, got = cut((keep, got), b, bit_of(b)), swap(send, 1 << b)
        total, send = add(keep, got)
        sums.append((total, swap(send, span, lambda t: not matched(t))))
        return [send]

    turn = settle(0)
    turn = settle(1)
    moved.append(swap(after(more_sends[1], *turn), 2))
    turn += [came[2], sums[0][1]]
    turn = settle(2)
    turn += [sums[1][1]]
    turn = settle(3)
    late = {0: jnp.stack([after(x, *turn) for x in came])}
    spread(late, outer_bits)

    olds = [
        lax.dynamic_slice(
            fast_weights, (head_of(plane, heads), 0, first[g] * share, 0), (1, 3, share, width)
        )
        for g in range(2)
    ]
    held = []
    for g in range(2):
        low = (after(sums[g][0], *turn), sums[g][1])
        send, keep = hand_over(low, sums[2 + g], span)
        held.append((keep, swap(send, 2 * span, matched)))
        turn = [send]
    turn += early.values()
    fresh = renew(after(held[0][0], *turn), held[0][1], olds[0], steps, span, heads)
    fresh = renew(*held[1], olds[1], steps, span, heads, fresh)
    turn = [fresh]
    for b in reversed(inner_bits[1:]):
        other = swap(fresh, 1 << b, matched)
        fresh = jnp.where(
            bit_of(b) == 1,
            jnp.concatenate([other, fresh], axis=2),
            jnp.concatenate([fresh, other], axis=2),
        )
    far = swap(fresh, 2, matched)
    late = {n: x if n == 0 else after(x, *turn) for n, x in late.items()}
    spread(late, [0])

    pieces, slots = [], {}
    for e in sorted(early):
        slots[e] = (len(pieces), None)
        pieces.append(early[e])
        for step in range(1, heads):
            slots[step * span + e] = (len(pieces), step - 1)
        pieces.append(late[e])
    slots = [slots[n] for n in range(count)]
    rows = arrange([after(pieces[0], *turn), *pieces[1:]], slots, span, heads, width)
    attended = attend(rows)
    far = after(far, attended)
    weights = [fresh, far, swap(fresh, 1, matched), swap(far, 1, matched)]
    split = heads // 2
    far_blocks = finish(rows, attended, weights, span, heads, tuple(range(split, heads)))
    got = [swap(x, (split + n) * span) for n, x in enumerate(far_blocks)]
    near_blocks = finish(
        after(rows, far_blocks[0]), attended, weights, span, heads, tuple(range(split))
    )
    got = [swap(x, step * span) if step else x for step, x in enumerate(near_blocks)] + got
    return join(got, span, heads, width)


def solution(mesh):
    rows = P(("groups", "tokens"), None)
    return jax.shard_map(
        on_device,
        mesh=mesh,
        in_specs=(
            rows,
            rows,
            rows,
            P(("groups", "tokens")),
            P(),
            P(),
            rows,
            rows,
            rows,
            P(("groups", "tokens")),
        ),
        out_specs=rows,
        check_vma=False,
    )
```

```python
import functools

import jax
import jax.numpy as jnp
from jax import lax
from jax.experimental import pallas as pl
from jax.experimental.pallas import tpu as pltpu
from jax.sharding import PartitionSpec as P

VIEW_ROWS = 128
AXIS = "tokens"
epsilon = 1e-05
f32 = jnp.float32
bf16 = jnp.bfloat16
i32 = jnp.int32
TAG_ROWS = 16
MIB = 1024 * 1024


def swap(value, mask, senders=None):
    count = lax.axis_size(AXIS)
    pairs = [(t, t ^ mask) for t in range(count) if senders is None or senders(t)]
    return lax.ppermute(value, AXIS, pairs)


def after(value, *others):
    return lax.optimization_barrier((value, *others))[0]


def head_of(plane, head_count):
    half = head_count // 2
    return (plane % 2) * half + plane // 2


def whole(shape):
    return pl.BlockSpec(shape, lambda i: (0,) * len(shape))


def position(span, heads):
    me = lax.axis_index(AXIS)
    plane, inner = me // span, me % span
    core = me % 2
    return (
        plane,
        core,
        (me // 2) % 2,
        me,
        inner,
        head_of(plane, heads),
        (plane % 2 == core).astype(i32),
    )


def call(body, name, inputs, specs, outs, out_specs=None, scratch=(), vmem=8, flops=0):
    return pl.pallas_call(
        body,
        name=name,
        grid=(1,),
        in_specs=specs,
        out_specs=out_specs or [whole(o.shape) for o in outs],
        scratch_shapes=list(scratch),
        out_shape=list(outs),
        cost_estimate=pl.CostEstimate(flops=flops, bytes_accessed=0, transcendentals=0),
        compiler_params=pltpu.CompilerParams(vmem_limit_bytes=vmem * MIB),
    )(*inputs)


def fetch_small(sources, buffers, sem):
    copies = [
        pltpu.make_async_copy(source, to, sem.at[n])
        for n, (source, to) in enumerate(zip(sources, buffers))
    ]
    for copy in copies:
        copy.start()
    return copies


def rate_column(rates, mask, head):
    at = lax.broadcasted_iota(i32, rates.shape, 0) == head
    row = jnp.sum(jnp.where(at, rates, 0.0), axis=0, keepdims=True) * mask.astype(f32)
    return -jnp.transpose(jnp.broadcast_to(row, (8, row.shape[1])))[:, 0:1]


def pack_body(span, heads, rates, mask, views, keys, values, *refs):
    half = heads // 2
    target, refs = refs[:3], refs[3:]
    packed, sent = refs[:half], refs[half : half + heads]
    rates_s, mask_s, views_s, value_s, pack_s, sent_s, in_sem, target_sem, out_sem = refs[
        half + heads :
    ]
    where = position(span, heads)
    rows, width = value_s.shape[1:]
    count = target[0].shape[0]

    def columns(head):
        return pl.ds(pl.multiple_of(head * width, width), width)

    small = fetch_small((rates, mask, views), (rates_s, mask_s, views_s), in_sem.at[half])
    loads = []
    for j in range(half):
        head = (1 - where[1]) * half + j
        for i, to in ((1, value_s.at[j]), (0, pack_s.at[j, 0])):
            source = (keys, values)[i]
            loads.append(pltpu.make_async_copy(source.at[:, columns(head)], to, in_sem.at[j, i]))
            loads[-1].start()
    rows_in = []
    for step in range(heads):
        head = head_of(where[0] ^ step, heads)
        for i in range(3):
            to = sent_s.at[step, pl.ds(i * count, count)]
            rows_in.append(
                pltpu.make_async_copy(
                    target[i].at[:, columns(head)], to, target_sem.at[step, i]
                )
            )
            rows_in[-1].start()
    for copy in small:
        copy.wait()
    row_at = lax.broadcasted_iota(i32, (TAG_ROWS, count), 0)
    ids = views_s[...]
    digits = jnp.where(row_at == 0, ids // 256, jnp.where(row_at == 1, ids % 256, 0))
    for step in range(heads):
        sent_s[step, pl.ds(3 * count, TAG_ROWS), :] = jnp.zeros((TAG_ROWS, width), bf16)
        sent_s[step, pl.ds(3 * count, TAG_ROWS), pl.ds(0, count)] = digits.astype(f32).astype(bf16)
    stores = []
    for j in range(half):
        rate = rate_column(rates_s[...], mask_s[...], (1 - where[1]) * half + j)
        loads[2 * j].wait()
        pack_s[j, 1] = (rate * value_s[j].astype(f32)).astype(bf16)
        loads[2 * j + 1].wait()
        stores.append(pltpu.make_async_copy(pack_s.at[j], packed[j], out_sem.at[j]))
        stores[-1].start()
    for step in range(heads):
        for i in range(3):
            rows_in[3 * step + i].wait()
        stores.append(pltpu.make_async_copy(sent_s.at[step], sent[step], out_sem.at[half + step]))
        stores[-1].start()
    for store in stores:
        store.wait()


def pack(rates, mask, views, keys, values, target, span, heads, width):
    half, rows, count = heads // 2, keys.shape[0], views.shape[1]
    small = (rates, mask, views)
    anywhere = pl.BlockSpec(memory_space=pl.ANY)
    piece = (3 * count + TAG_ROWS, width)
    outs = call(
        functools.partial(pack_body, span, heads),
        "pack",
        (*small, keys, values, *target),
        [anywhere] * 8,
        [jax.ShapeDtypeStruct((2, rows, width), bf16)] * half
        + [jax.ShapeDtypeStruct(piece, bf16)] * heads,
        out_specs=[anywhere] * (half + heads),
        scratch=[
            *[pltpu.VMEM(x.shape, x.dtype) for x in small],
            pltpu.VMEM((half, rows, width), bf16),
            pltpu.VMEM((half, 2, rows, width), bf16),
            pltpu.VMEM((heads, *piece), bf16),
            pltpu.SemaphoreType.DMA((half + 1, 3)),
            pltpu.SemaphoreType.DMA((heads, 3)),
            pltpu.SemaphoreType.DMA((half + heads,)),
        ],
        vmem=62,
    )
    return outs[:half], outs[half:]


def head_grad_body(span, heads, lane, rates, mask, keys, values, other, weights, *refs):
    rates_s, mask_s, k_s, v_s, w_s, tg_s, hidden_s, gate_s, up_s, full, send_s, keep_s = refs[-14:-2]
    in_sem, out_sem = refs[-2:]
    outs = refs[:-14]
    arrays = len(outs) // 2
    sends, keeps = outs[:arrays], outs[arrays:]
    rows, width = v_s.shape
    where = position(span, heads)
    head = where[1] * (heads // 2) + lane
    cols = pl.ds(pl.multiple_of(head * width, width), width)
    upper, lower = pl.ds(0, rows), pl.ds(rows, rows)
    loads = [
        pltpu.make_async_copy(keys.at[:, cols], k_s.at[upper], in_sem.at[0]),
        pltpu.make_async_copy(weights.at[head, 0], w_s.at[0], in_sem.at[1]),
        pltpu.make_async_copy(weights.at[head, 1], w_s.at[1], in_sem.at[2]),
        pltpu.make_async_copy(values.at[:, cols], v_s, in_sem.at[3]),
        pltpu.make_async_copy(weights.at[head, 2], w_s.at[2], in_sem.at[4]),
        pltpu.make_async_copy(other.at[0], k_s.at[lower], in_sem.at[5]),
        pltpu.make_async_copy(other.at[1], tg_s.at[lower], in_sem.at[6]),
    ]
    small = fetch_small((rates, mask), (rates_s, mask_s), in_sem.at[pl.ds(7, 2)])
    for load in loads[:2]:
        load.start()
    for copy in small:
        copy.wait()
    for load in loads[2:]:
        load.start()
    rate = rate_column(rates_s[...], mask_s[...], head)
    chunk = 256
    for at in range(0, 2 * rows, chunk):
        span = pl.ds(at, chunk)
        if at == 0:
            loads[0].wait()
            loads[1].wait()
        if at == rows:
            loads[5].wait()
        k = k_s[span, :]
        pre_gate = jnp.dot(k, w_s[0], preferred_element_type=f32)
        if at == 0:
            loads[2].wait()
        pre_up = jnp.dot(k, w_s[1], preferred_element_type=f32)
        if at == 0:
            loads[3].wait()
            loads[4].wait()
        if at == rows:
            loads[6].wait()
        if at < rows:
            tg = (rate[at : at + chunk] * v_s[span, :].astype(f32)).astype(bf16)
            tg_s[span, :] = tg
        else:
            tg = tg_s[span, :]
        back = lax.dot_general(tg, w_s[2], (((1,), (1,)), ((), ())), preferred_element_type=f32)
        sigma = 0.5 * jnp.tanh(0.5 * pre_gate) + 0.5
        activated = pre_gate * sigma
        hidden_s[span, :] = (activated * pre_up).astype(bf16)
        gate_s[span, :] = (back * pre_up * (sigma + activated * (1.0 - sigma))).astype(bf16)
        up_s[span, :] = (back * activated).astype(bf16)
    quarter = width // 4
    bit = where[2]
    stores = []
    for i, left, right in ((2, hidden_s, tg_s), (0, k_s, gate_s), (1, k_s, up_s)):
        full[...] = lax.dot_general(
            left[...], right[...], (((0,), (0,)), ((), ())), preferred_element_type=f32
        )
        for g in range(2):
            kept = pl.ds(pl.multiple_of(bit * 2 * quarter + g * quarter, quarter), quarter)
            sent = pl.ds(pl.multiple_of((1 - bit) * 2 * quarter + g * quarter, quarter), quarter)
            send_s[g, i] = full[sent, :].astype(bf16)
            keep_s[g, i] = full[kept, :]
            stores += [
                pltpu.make_async_copy(
                    send_s.at[g, i], sends[g % arrays].at[g // arrays, i], out_sem.at[0, g, i]
                ),
                pltpu.make_async_copy(
                    keep_s.at[g, i], keeps[g % arrays].at[g // arrays, i], out_sem.at[1, g, i]
                ),
            ]
            stores[-2].start()
            stores[-1].start()
    for store in stores:
        store.wait()


def head_grad(rates, mask, keys, values, other, weights, span, heads, lane, width, arrays):
    rows = keys.shape[0]
    shape = (3, width // 4, width)
    out = (2 // arrays, *shape)
    anywhere = pl.BlockSpec(memory_space=pl.ANY)
    in_hbm = pl.BlockSpec(memory_space=pltpu.HBM)
    both = pltpu.VMEM((2 * rows, width), bf16)
    outs = call(
        functools.partial(head_grad_body, span, heads, lane),
        "head_grad_%d" % lane,
        (rates, mask, keys, values, other, weights),
        [anywhere, anywhere, in_hbm, in_hbm, anywhere, in_hbm],
        [jax.ShapeDtypeStruct(out, bf16)] * arrays + [jax.ShapeDtypeStruct(out, f32)] * arrays,
        out_specs=[anywhere] * 2 * arrays,
        scratch=[
            pltpu.VMEM(rates.shape, f32),
            pltpu.VMEM(mask.shape, i32),
            both,
            pltpu.VMEM((rows, width), bf16),
            pltpu.VMEM((3, width, width), bf16),
            both,
            both,
            both,
            both,
            pltpu.VMEM((width, width), f32),
            pltpu.VMEM((2, *shape), bf16),
            pltpu.VMEM((2, *shape), f32),
            pltpu.SemaphoreType.DMA((9,)),
            pltpu.SemaphoreType.DMA((2, 2, 3)),
        ],
        vmem=62,
    )
    return outs[:arrays], outs[arrays:]


def arrange_body(slots, span, *refs):
    out = refs[-1]
    pieces = []
    for n, at in slots:
        pieces.append(refs[n] if at is None else refs[n].at[at])
    me = lax.axis_index(AXIS)
    inner = me % span
    rows = (pieces[0].shape[0] - TAG_ROWS) // 3
    count = len(pieces)
    heads = count // span
    tags = [p[pl.ds(3 * rows, TAG_ROWS), pl.ds(0, rows)].astype(f32) for p in pieces]
    ids = jnp.concatenate([t[0:1, :] * 256.0 + t[1:2, :] for t in tags], axis=0).astype(i32)
    square = (count, count)
    earlier = (
        (me ^ lax.broadcasted_iota(i32, square, 1)) < (me ^ lax.broadcasted_iota(i32, square, 0))
    ).astype(f32)
    before = (
        lax.broadcasted_iota(i32, (rows, rows), 0) < lax.broadcasted_iota(i32, (rows, rows), 1)
    ).astype(f32)
    place = jnp.full((count, rows), -1.0, f32)
    for j in range(heads):
        hit = (ids == j * span + inner).astype(f32)
        rank = jnp.dot(hit, before, preferred_element_type=f32) + jnp.sum(
            jnp.dot(earlier, hit, preferred_element_type=f32), axis=1, keepdims=True
        )
        place = jnp.where(hit > 0.0, rank + float(j * VIEW_ROWS), place)
    place = place.astype(i32)
    group = 4
    totals = [None] * 3
    for first in range(0, count, group):
        row_at = lax.broadcasted_iota(i32, (heads * VIEW_ROWS, rows), 0)
        pick = jnp.concatenate(
            [
                (row_at == place[n : n + 1, :]).astype(f32).astype(bf16)
                for n in range(first, first + group)
            ],
            axis=1,
        )
        for i in range(3):
            source = jnp.concatenate(
                [pieces[n][pl.ds(i * rows, rows), :] for n in range(first, first + group)],
                axis=0,
            )
            part = jnp.dot(pick, source, preferred_element_type=f32)
            totals[i] = part if totals[i] is None else totals[i] + part
    for i in range(3):
        out[i] = totals[i].astype(bf16)


def arrange(pieces, slots, span, heads, width):
    return call(
        functools.partial(arrange_body, slots, span),
        "arrange",
        tuple(pieces),
        [whole(x.shape) for x in pieces],
        [jax.ShapeDtypeStruct((3, heads * VIEW_ROWS, width), bf16)],
        vmem=20,
    )[0]


def attend_body(rows, attended):
    width = rows.shape[2]
    for v in range(rows.shape[1] // VIEW_ROWS):
        at = pl.ds(v * VIEW_ROWS, VIEW_ROWS)
        scores = lax.dot_general(
            rows[0, at, :], rows[1, at, :], (((1,), (1,)), ((), ())), preferred_element_type=f32
        ) * width ** (-0.5)
        top = jnp.max(scores, axis=1, keepdims=True)
        raised = jnp.exp(scores - top)
        probs = (raised / jnp.sum(raised, axis=1, keepdims=True)).astype(bf16)
        attended[at, :] = jnp.dot(probs, rows[2, at, :], preferred_element_type=f32)


def attend(rows):
    return call(
        attend_body,
        "attend",
        (rows,),
        [whole(rows.shape)],
        [jax.ShapeDtypeStruct(rows.shape[1:], f32)],
    )[0]


def add_body(keep, got, total, send):
    total[...] = keep[...] + got[...].astype(f32)
    send[...] = total[...].astype(bf16)


def add(keep, got):
    return call(
        add_body,
        "add",
        (keep, got),
        [whole(keep.shape)] * 2,
        [jax.ShapeDtypeStruct(keep.shape, t) for t in (f32, bf16)],
        flops=2000000000,
    )


def pick_body(span, kept, *refs):
    sources, out, total_s, got_s, sem = refs[:4], *refs[4:]
    upper = lax.axis_index(AXIS) // span // 2 == 1

    def fetch(pair):
        copies = [
            pltpu.make_async_copy(source, to, sem.at[n])
            for n, (source, to) in enumerate(zip(pair, (total_s, got_s)))
        ]
        for copy in copies:
            copy.start()
        for copy in copies:
            copy.wait()

    @pl.when(upper)
    def _():
        fetch(sources[2:] if kept else sources[:2])

    @pl.when(jnp.logical_not(upper))
    def _():
        fetch(sources[:2] if kept else sources[2:])

    out[...] = (total_s[...] + got_s[...].astype(f32)).astype(out.dtype)


def pick(low, high, span, kept):
    shape = low[0].shape
    return call(
        functools.partial(pick_body, span, kept),
        "keep" if kept else "hand_over",
        (*low, *high),
        [pl.BlockSpec(memory_space=pl.ANY)] * 4,
        [jax.ShapeDtypeStruct(shape, f32 if kept else bf16)],
        scratch=[
            pltpu.VMEM(shape, f32),
            pltpu.VMEM(shape, bf16),
            pltpu.SemaphoreType.DMA((2,)),
        ],
        flops=0 if kept else 4000000000,
    )[0]


def renew_body(span, heads, keep, got, old, steps, *refs):
    *earlier, fresh = refs
    step = jnp.where(
        lax.broadcasted_iota(i32, steps.shape, 1) == position(span, heads)[5], steps[...], 0.0
    )
    step = jnp.sum(step, axis=1, keepdims=True)
    total = keep[...] + got[...].astype(f32)
    scale = lax.rsqrt(jnp.mean(total * total, axis=-1, keepdims=True) + epsilon)
    new = (old[...].astype(f32) - step * (total * scale)).astype(bf16)
    if earlier:
        fresh[pl.ds(0, 1)] = earlier[0][...]
        fresh[pl.ds(1, 1)] = new
    else:
        fresh[...] = new


def renew(keep, got, old, steps, span, heads, *earlier):
    shape = (keep.shape[0] + len(earlier), *keep.shape[1:])
    inputs = (keep, got, old, steps, *earlier)
    return call(
        functools.partial(renew_body, span, heads),
        "renew_%d" % len(earlier),
        inputs,
        [whole(x.shape) for x in inputs],
        [jax.ShapeDtypeStruct(shape, bf16)],
    )[0]


def finish_body(span, heads, steps, rows, attended, *refs):
    weights = refs[:4]
    outs, full = refs[4:-1], refs[-1]
    where = position(span, heads)
    bit, is_owner = where[2], where[6]
    quarter = weights[0].shape[2]

    def place(blocks):
        for side, block in enumerate(blocks):
            half = bit if side == 0 else 1 - bit
            for g in range(2):
                at = pl.ds(pl.multiple_of(half * 2 * quarter + g * quarter, quarter), quarter)
                for i in range(3):
                    full[i, at, :] = block[g, i]

    @pl.when(is_owner == 1)
    def _():
        place(weights[:2])

    @pl.when(is_owner == 0)
    def _():
        place(weights[2:])

    for step, out in zip(steps, outs):
        at = pl.ds(pl.multiple_of((where[0] ^ step) * VIEW_ROWS, VIEW_ROWS), VIEW_ROWS)
        q = rows[0, at, :]
        pre_gate = jnp.dot(q, full[0], preferred_element_type=f32)
        pre_up = jnp.dot(q, full[1], preferred_element_type=f32)
        hidden = (pre_gate * jax.nn.sigmoid(pre_gate) * pre_up).astype(bf16)
        fast = jnp.dot(hidden, full[2], preferred_element_type=f32)
        scale = lax.rsqrt(jnp.mean(fast * fast, axis=-1, keepdims=True) + epsilon)
        out[...] = (fast * scale + attended[at, :]).astype(bf16)


def finish(rows, attended, weights, span, heads, steps):
    width = rows.shape[2]
    inputs = (rows, attended, *weights)
    return call(
        functools.partial(finish_body, span, heads, steps),
        "finish_%d" % steps[0],
        inputs,
        [pl.BlockSpec((1, *rows.shape[1:]), lambda i: (0, 0, 0))]
        + [whole(x.shape) for x in inputs[1:]],
        [jax.ShapeDtypeStruct((VIEW_ROWS, width), bf16)] * len(steps),
        scratch=[pltpu.VMEM((3, width, width), bf16)],
        vmem=12,
    )


def join_body(span, heads, width, *refs):
    out = refs[-1]
    plane = lax.axis_index(AXIS) // span
    for step in range(heads):
        head = head_of(plane ^ step, heads)
        out[:, pl.ds(pl.multiple_of(head * width, width), width)] = refs[step][...]


def join(blocks, span, heads, width):
    rows = blocks[0].shape[0]
    return call(
        functools.partial(join_body, span, heads, width),
        "join",
        tuple(blocks),
        [whole(x.shape) for x in blocks],
        [jax.ShapeDtypeStruct((rows, heads * width), bf16)],
    )[0]


def on_device(
    update_keys,
    update_values,
    update_rates,
    update_mask,
    fast_weights,
    step_sizes,
    target_queries,
    target_keys,
    target_values,
    target_views,
):
    heads, _, width, _ = fast_weights.shape
    half = heads // 2
    count = lax.axis_size(AXIS)
    me = lax.axis_index(AXIS)
    span = count // heads
    plane, inner = me // span, me % span
    core = inner % 2
    inner_bits = list(range(1, span.bit_length() - 1))
    bit_of = lambda b: (me >> b) & 1
    matched = lambda t: (t // span) % 2 == t % 2

    share = width // 4 // 2 ** (len(inner_bits) - 1)
    first = [bit_of(1) * 2 + g for g in range(2)]
    for b in inner_bits[1:]:
        first = [2 * f + bit_of(b) for f in first]

    rates, mask = update_rates.T, update_mask[None, :]
    steps = step_sizes[None, :]

    others, sent = pack(
        rates,
        mask,
        target_views[None, :],
        update_keys,
        update_values,
        (target_queries, target_keys, target_values),
        span,
        heads,
        width,
    )
    turn = [sent[0]]
    others = [swap(x, 1) for x in others]

    outer_bits = list(reversed(inner_bits))

    def spread(parts, bits):
        for b in bits:
            parts.update({n | (1 << b): swap(x, 1 << b) for n, x in list(parts.items())})

    early = {0: sent[0]}
    spread(early, outer_bits)
    came = [swap(sent[step], step * span) for step in (1, 2)]

    grad_inputs = (mask, update_keys, update_values)
    sends, keeps = head_grad(
        after(rates, *turn), *grad_inputs, others[0], fast_weights, span, heads, 0, width, 2
    )
    turn = [sends[0], *early.values()]
    spread(early, [0])
    more_sends, more_keeps = head_grad(
        after(rates, *turn), *grad_inputs, others[1], fast_weights, span, heads, 1, width, 2
    )
    turn = [more_sends[0], *came]
    keeps = [*keeps, *more_keeps]
    moved = [
        swap(sends[0], 2),
        swap(after(sends[1], more_sends[0]), 2),
        swap(after(more_sends[0], *turn[1:]), 2),
    ]
    came.append(swap(after(sent[3], *turn), 3 * span))

    def cut(pair, b, side):
        rows = pair[0].shape[2] // 2
        return sum(
            lax.dynamic_slice_in_dim(x, side * rows, rows, 2).astype(f32) for x in pair
        )

    sums = []

    def settle(n):
        keep, got = keeps[n], after(moved[n], *turn)
        for b in inner_bits[1:]:
            send = cut((keep, got), b, 1 - bit_of(b)).astype(bf16)
            keep, got = cut((keep, got), b, bit_of(b)), swap(send, 1 << b)
        total, send = add(keep, got)
        sums.append((total, swap(send, span, lambda t: not matched(t))))
        return [send]

    turn = settle(0)
    turn = settle(1)
    moved.append(swap(after(more_sends[1], *turn), 2))
    turn += [came[2], sums[0][1]]
    turn = settle(2)
    turn += [sums[1][1]]
    turn = settle(3)
    late = {0: jnp.stack([after(x, *turn) for x in came])}
    spread(late, outer_bits)

    olds = [
        lax.dynamic_slice(
            fast_weights, (head_of(plane, heads), 0, first[g] * share, 0), (1, 3, share, width)
        )
        for g in range(2)
    ]
    held = []
    for g in range(2):
        low = (after(sums[g][0], *turn), sums[g][1])
        send = pick(low, sums[2 + g], span, False)
        held.append(swap(send, 2 * span, matched))
        turn = [send]
    held = [
        (pick((after(sums[g][0], *turn), sums[g][1]), sums[2 + g], span, True), got)
        for g, got in enumerate(held)
    ]
    turn += early.values()
    fresh = renew(after(held[0][0], *turn), held[0][1], olds[0], steps, span, heads)
    fresh = renew(*held[1], olds[1], steps, span, heads, fresh)
    turn = [fresh]
    for b in reversed(inner_bits[1:]):
        other = swap(fresh, 1 << b, matched)
        fresh = jnp.where(
            bit_of(b) == 1,
            jnp.concatenate([other, fresh], axis=2),
            jnp.concatenate([fresh, other], axis=2),
        )
    far = swap(fresh, 2, matched)
    late = {n: x if n == 0 else after(x, *turn) for n, x in late.items()}
    spread(late, [0])

    pieces, slots = [], {}
    for e in sorted(early):
        slots[e] = (len(pieces), None)
        pieces.append(early[e])
        for step in range(1, heads):
            slots[step * span + e] = (len(pieces), step - 1)
        pieces.append(late[e])
    slots = [slots[n] for n in range(count)]
    rows = arrange([after(pieces[0], *turn), *pieces[1:]], slots, span, heads, width)
    attended = attend(rows)
    far = after(far, attended)
    weights = [fresh, far, swap(fresh, 1, matched), swap(far, 1, matched)]
    split = heads // 2
    far_blocks = finish(rows, attended, weights, span, heads, tuple(range(split, heads)))
    got = [swap(x, (split + n) * span) for n, x in enumerate(far_blocks)]
    near_blocks = finish(
        after(rows, far_blocks[0]), attended, weights, span, heads, tuple(range(split))
    )
    got = [swap(x, step * span) if step else x for step, x in enumerate(near_blocks)] + got
    return join(got, span, heads, width)


def solution(mesh):
    rows = P(("groups", "tokens"), None)
    return jax.shard_map(
        on_device,
        mesh=mesh,
        in_specs=(
            rows,
            rows,
            rows,
            P(("groups", "tokens")),
            P(),
            P(),
            rows,
            rows,
            rows,
            P(("groups", "tokens")),
        ),
        out_specs=rows,
        check_vma=False,
    )
```
